32 devices in a mesh: grp: 4 (over z), dev: 8 (over y, x, core).
Axes of the slice: x: 2, y: 2, z: 4, core: 2. Of those that a mesh axis runs over, the one named last changes fastest.
Arguments:
- columns: float32 [16384, 768], P(('grp', 'dev')), may hold values from -6 to 6
- points: float32 [3, 16384], P(None, ('grp', 'dev')), may hold values from 0 to 1, as said below
- basis: float32 [16384, 128], P(('grp', 'dev')), may hold values from -0.25 to 0.25
- transfer: float32 [32, 128, 128], P(('grp', 'dev')), may hold values from -0.5 to 0.5
- leaf_coupling: float32 [32, 4, 128, 128], P(('grp', 'dev')), may hold values from -0.5 to 0.5
- group_coupling: float32 [4, 4, 128, 128], P('grp', None, 'dev'), may hold values from -0.25 to 0.25
- near_pairs: int32 [32, 3], replicated, may hold values from 0 to 1, as said below
- far_mask: int32 [32, 4], P(('grp', 'dev')), may hold values 0 or 1
- group_link_mask: int32 [4, 4], P('grp'), may hold values 0 or 1
Outputs:
- product: float32 [16384, 768], P(('grp', 'dev'))
The draws below stay inside these ranges and needn't reach their ends.
Inputs may be any that keep to these rules, and one draw needn't show every extreme that they name: `near_pairs`: each row is a run of ones followed by zeros; some row is all ones. First coordinate of leaf i's points lies in [i / 32, (i + 1) / 32); all coordinates lie in [0, 1).
All inputs are finite; a program needn't handle non-finite values. No bound on the sum of `far_mask` or of `group_link_mask` on one device may be relied on, other than what follows from the above.
Results may differ from the reference program's by a relative error of at most 0.0003.
Values sent between devices are 32-bit elements; how exact they have to be, the bound alone decides.
A program may use at most 64 MiB of HBM per device.

```python
import math
import jax
import jax.numpy as jnp
from jax import lax

LEAF = 512
COLS = 768
RANK = 128
NEAR_REACH = 3
FAR_REACH = 2
GROUPS = 4
PER_GROUP = 8
LEAVES = 32
TOTAL = 16384


def draw_points(key, part):
    first_key, rest_key = jax.random.split(jax.random.fold_in(key, 11))
    owner = (jnp.arange(TOTAL) // LEAF).astype(jnp.float32)
    inside = jax.random.uniform(first_key, (TOTAL,), jnp.float32, 0.0, 0.999)
    first = (owner + inside) / LEAVES
    rest = jax.random.uniform(rest_key, (2, TOTAL), jnp.float32, 0.0, 0.999)
    return jnp.concatenate([first[None, :], rest], axis=0)


def draw_near_pairs(key, part):
    count_key, gate_key, place_key = jax.random.split(jax.random.fold_in(key, 23), 3)
    counts = jax.random.randint(count_key, (LEAVES,), 0, NEAR_REACH + 1)
    counts = counts * jax.random.randint(gate_key, (LEAVES,), 0, 2)
    where = jax.random.randint(place_key, (), 0, LEAVES)
    counts = jnp.where(jnp.arange(LEAVES) == where, NEAR_REACH, counts)
    outward_steps = jnp.arange(1, NEAR_REACH + 1)
    return (outward_steps[None, :] <= counts[:, None]).astype(jnp.int32)


def place_ends(entries, stream_key, least, top_value):
    shape = entries.shape
    spot = [jax.random.randint(jax.random.fold_in(stream_key, axis), (), 0, shape[axis]) for axis in range(len(shape))]
    entries = entries.at[tuple(spot)].set(least)
    longest = shape.index(max(shape))
    spot[longest] = (spot[longest] + 1) % shape[longest]
    return entries.at[tuple(spot)].set(top_value)


def levels(rng, dims, pieces, low, high):
    factor_of, own = 1.0, jax.random.fold_in(rng, 6)
    for position, shards_of in pieces:
        heights = jnp.exp(jax.random.uniform(jax.random.fold_in(own, position), (shards_of,), jnp.float32, low / len(pieces), high / len(pieces)))
        factor_of = factor_of * jnp.repeat(heights, dims[position] // shards_of).reshape([-1 if axis == position else 1 for axis in range(len(dims))])
    return factor_of


def normal_values(key, dims, width, most, cuts=(), dtype=jnp.bfloat16):
    drawn = jax.random.normal(key, dims, jnp.float32) * width
    if len(cuts) > 0:
        drawn = levels(key, dims, cuts, -0.22, 0.18) * drawn
    return jnp.clip(drawn, min=-most, max=most).astype(dtype)


def setup_inputs(seed: int = 0) -> dict:
    splits = jax.random.split(jax.random.key(seed), 10)
    columns = normal_values(splits[0], (TOTAL, COLS), 1.0, 6.0, ((0, 32),), jnp.float32)
    points = draw_points(jax.random.fold_in(splits[9], 71), 0)
    basis = normal_values(splits[2], (TOTAL, RANK), LEAF ** -0.5, 0.25, ((0, 32),), jnp.float32)
    transfer = normal_values(splits[3], (LEAVES, RANK, RANK), RANK ** -0.5, 0.5, ((0, 32),), jnp.float32)
    leaf_coupling = normal_values(splits[4], (LEAVES, 2 * FAR_REACH, RANK, RANK), RANK ** -0.5, 0.5, ((0, 32),), jnp.float32)
    group_coupling = normal_values(splits[5], (GROUPS, GROUPS, RANK, RANK), (RANK * GROUPS) ** -0.5, 0.25, ((0, 4), (2, 8)), jnp.float32)
    near_pairs = draw_near_pairs(jax.random.fold_in(splits[9], 71), 0)
    far_mask = place_ends((jax.random.randint(splits[7], (LEAVES, 2 * FAR_REACH), 0, 4) < 3).astype(jnp.int32), jax.random.fold_in(splits[7], 1), 0, 1)
    group_link_mask = place_ends((jax.random.randint(splits[8], (GROUPS, GROUPS), 0, 4) < 3).astype(jnp.int32), jax.random.fold_in(splits[8], 1), 0, 1)
    return {"columns": columns, "points": points, "basis": basis, "transfer": transfer, "leaf_coupling": leaf_coupling, "group_coupling": group_coupling, "near_pairs": near_pairs, "far_mask": far_mask, "group_link_mask": group_link_mask}


soften_sq = 0.0025
dense_result = lax.Precision.HIGHEST

def kernel(targets, sources):
    delta = targets[:, :, None] - sources[:, None, :]
    delta = delta - jnp.floor(delta + 0.5)
    squared = lax.optimization_barrier(jnp.sum(delta * delta, axis=0))
    return lax.rsqrt(squared + soften_sq) * (1.0 / math.sqrt(targets.shape[1]))

def product_of(left, right):
    return jnp.dot(left, right, precision=dense_result)

def nearfield_block(targets, sources, values):
    return product_of(kernel(targets, sources), values)

def no_block(targets, sources, values):
    return jnp.zeros((targets.shape[1], values.shape[1]), jnp.float32)

def reference(columns, points, basis, transfer, leaf_coupling, group_coupling, near_pairs, far_mask, group_link_mask):
    leaves = LEAVES
    leaf_cols = columns.reshape(leaves, LEAF, COLS)
    leaf_points = points.reshape(3, leaves, LEAF).transpose(1, 0, 2)
    leaf_basis = basis.reshape(leaves, LEAF, RANK)
    expansion_weights = jnp.einsum('lnr,lnc->lrc', leaf_basis, leaf_cols, precision=dense_result)
    raised_values = jnp.einsum('vxz,vxq->vzq', transfer, expansion_weights, precision=dense_result)
    cluster = raised_values.reshape(GROUPS, PER_GROUP, RANK, COLS).sum(axis=1)
    weights = group_link_mask.astype(jnp.float32)
    group_far = jnp.einsum('gh,ghba,hbc->gac', weights, group_coupling, cluster, precision=dense_result)
    leaf_far = jnp.zeros((leaves, RANK, COLS), jnp.float32)
    for entry in range(2 * FAR_REACH):
        distance = NEAR_REACH + 1 + entry // 2
        partner = -distance if entry % 2 == 0 else distance
        moved = jnp.roll(expansion_weights, -partner, axis=0)
        scaled = far_mask[:, entry].astype(jnp.float32)[:, None, None]
        leaf_far = leaf_far + scaled * jnp.einsum('lab,lbc->lac', leaf_coupling[:, entry], moved, precision=dense_result)
    distributed_values = jnp.repeat(group_far, PER_GROUP, axis=0)
    total = leaf_far + jnp.einsum('lab,lbc->lac', transfer, distributed_values, precision=dense_result)
    far_rows = jnp.einsum('lnr,lrc->lnc', leaf_basis, total, precision=dense_result)

    def one_leaf(index):
        result = nearfield_block(leaf_points[index], leaf_points[index], leaf_cols[index])
        for distance in range(1, NEAR_REACH + 1):
            upper = (index + distance) % leaves
            result = result + lax.cond(near_pairs[index, distance - 1] > 0, nearfield_block, no_block, leaf_points[index], leaf_points[upper], leaf_cols[upper])
            lower = (index - distance) % leaves
            result = result + lax.cond(near_pairs[lower, distance - 1] > 0, nearfield_block, no_block, leaf_points[index], leaf_points[lower], leaf_cols[lower])
        return result
    near = lax.map(one_leaf, jnp.arange(leaves))
    return (near + far_rows).reshape(TOTAL, COLS)
```

```python
import functools
import math

import jax
import jax.numpy as jnp
from jax import lax
from jax.experimental import pallas as pl
from jax.experimental.pallas import tpu as pltpu
from jax.sharding import PartitionSpec as P

soften_sq = 0.0025
chunks = 8
row_tile = 128
f32 = jnp.float32
MESH = pl.DeviceIdType.MESH


def slot_of(offset):
    return offset + 3 if offset < 0 else offset + 2


def halves(value):
    high = value.astype(jnp.bfloat16)
    return high, (value - high.astype(f32)).astype(jnp.bfloat16)


def dot16(left, right):
    return jnp.dot(left, right, preferred_element_type=f32)


def dot_split(left, right):
    lh, ll = left
    rh, rl = right
    return dot16(lh, rh) + dot16(lh, rl) + dot16(ll, rh)


def body(
    groups, peers, near_w, far_w, cols, pts, pts_t, basis, basis_t, up, up_t, coupling, links,
    out, slots, xh, xl, pown, pbuf, coef, cbuf, lift, lift_in, gath, part, part_in, far,
    s_send, s_recv, p_send, p_recv, c_send, c_recv, r_send, r_recv, g_send, g_recv,
    q_send, q_recv, f_send, f_recv,
):
    leaf, width = cols.shape
    leaves = groups * peers
    grp, dev = lax.axis_index("grp"), lax.axis_index("dev")
    me = grp * peers + dev
    place = lax.rem(me, 4)
    outer = (place == 0) | (place == 3)
    inner = (place == 1) | (place == 2)
    sign = 1 - 2 * (place // 2)
    step = leaf // chunks

    def device(index):
        index = lax.rem(index + leaves, leaves)
        return (index // peers, lax.rem(index, peers))

    barrier = pltpu.get_barrier_semaphore()
    for offset in (-4, -3, -2, -1, 1, 2, 3, 4):
        pl.semaphore_signal(barrier, inc=1, device_id=device(me + offset), device_id_type=MESH)

    @pl.loop(1, peers)
    def _(t):
        pl.semaphore_signal(
            barrier, inc=1, device_id=(grp, lax.rem(dev + t, peers)), device_id_type=MESH
        )

    @pl.loop(1, groups)
    def _(t):
        pl.semaphore_signal(
            barrier, inc=1, device_id=(lax.rem(grp + t, groups), dev), device_id_type=MESH
        )

    pl.semaphore_wait(barrier, 8 + peers - 1 + groups - 1)

    def piece(k):
        return pl.ds(pl.multiple_of(k * step, step), step)

    def relay(source, k, channel, to, offset):
        slot = slot_of(offset)
        return pltpu.make_async_remote_copy(
            src_ref=source.at[piece(k)],
            dst_ref=slots.at[slot, piece(k)],
            send_sem=s_send.at[channel, k],
            recv_sem=s_recv.at[slot, k],
            device_id=device(me + to * sign),
            device_id_type=MESH,
        )

    def arrived(slot, k):
        pltpu.make_async_remote_copy(
            src_ref=cols.at[piece(k)],
            dst_ref=slots.at[slot, piece(k)],
            send_sem=s_send.at[0, k],
            recv_sem=s_recv.at[slot, k],
            device_id=device(me + 1),
            device_id_type=MESH,
        ).wait_recv()

    def arrived_all(slot):
        @pl.loop(0, chunks)
        def _(k):
            arrived(slot, k)

    def own_outer(k):
        return (
            relay(cols, k, 0, 2, 2),
            relay(cols, k, 1, -3, 3),
            relay(cols, k, 2, 1, -1),
        )

    def own_inner(k):
        return (
            relay(cols, k, 0, 2, 2),
            relay(cols, k, 1, 3, -3),
            relay(cols, k, 2, -1, 1),
        )

    plus2, plus3 = slots.at[slot_of(2)], slots.at[slot_of(3)]
    minus1, minus2 = slots.at[slot_of(-1)], slots.at[slot_of(-2)]

    def first_outer(k):
        return relay(plus2, k, 3, 4, -2), relay(plus2, k, 4, 1, 1)

    def first_inner(k):
        return relay(plus3, k, 3, 2, -1), relay(plus2, k, 4, -1, 3)

    def later_outer(k):
        return relay(minus2, k, 5, 1, -3), relay(minus1, k, 6, 1, -2)

    def start_each(copies):
        for copy in copies:
            copy.start()

    @pl.when(outer)
    def _():
        @pl.loop(0, chunks)
        def _(k):
            start_each(own_outer(k))

    @pl.when(inner)
    def _():
        @pl.loop(0, chunks)
        def _(k):
            start_each(own_inner(k))

    pown[0:3, :] = pts[...]
    pown[3:8, :] = jnp.zeros((5, leaf), f32)

    def point_copy(offset):
        return pltpu.make_async_remote_copy(
            src_ref=pown,
            dst_ref=pbuf.at[slot_of(-offset)],
            send_sem=p_send.at[slot_of(offset)],
            recv_sem=p_recv.at[slot_of(-offset)],
            device_id=device(me + offset),
            device_id_type=MESH,
        )

    near_offsets = (-3, -2, -1, 1, 2, 3)
    for offset in near_offsets:
        point_copy(offset).start()

    def split_columns(source):
        @pl.loop(0, leaf // row_tile)
        def _(t):
            rows = pl.ds(pl.multiple_of(t * row_tile, row_tile), row_tile)
            high, low = halves(source[rows, :])
            xh[rows, :] = high
            xl[rows, :] = low

    split_columns(cols)
    coef[...] = dot_split(halves(basis_t[...]), (xh[...], xl[...]))

    def coef_copy(source, slot, to):
        return pltpu.make_async_remote_copy(
            src_ref=source,
            dst_ref=cbuf.at[slot],
            send_sem=c_send.at[slot],
            recv_sem=c_recv.at[slot],
            device_id=device(me + to),
            device_id_type=MESH,
        )

    coef_copies = (
        coef_copy(coef, 0, 4),
        coef_copy(coef, 1, -4),
        coef_copy(cbuf.at[0], 2, 1),
        coef_copy(cbuf.at[1], 3, -1),
    )
    coef_copies[0].start()
    coef_copies[1].start()

    def spread(source, target, send, recv, t):
        to = lax.rem(dev + t, peers)
        return pltpu.make_async_remote_copy(
            src_ref=source.at[to],
            dst_ref=target.at[dev],
            send_sem=send.at[t],
            recv_sem=recv.at[dev],
            device_id=(grp, to),
            device_id_type=MESH,
        )

    def collect(target, recv, t):
        origin = lax.rem(dev - t + peers, peers)
        pltpu.make_async_remote_copy(
            src_ref=lift.at[0],
            dst_ref=target.at[origin],
            send_sem=r_send.at[0],
            recv_sem=recv.at[origin],
            device_id=(grp, origin),
            device_id_type=MESH,
        ).wait_recv()
        return target[origin]

    def scatter_start(value, source, target, send, recv):
        source[...] = value.reshape(source.shape)

        @pl.loop(1, peers)
        def _(t):
            spread(source, target, send, recv, t).start()

    def scatter_end(source, target, recv):
        return lax.fori_loop(
            1, peers, lambda t, total: total + collect(target, recv, t), source[dev]
        )

    def group_copy(t):
        return pltpu.make_async_remote_copy(
            src_ref=gath.at[grp],
            dst_ref=gath.at[grp],
            send_sem=g_send.at[t],
            recv_sem=g_recv.at[grp],
            device_id=(lax.rem(grp + t, groups), dev),
            device_id_type=MESH,
        )

    def group_arrived(t):
        origin = lax.rem(grp - t + groups, groups)
        pltpu.make_async_remote_copy(
            src_ref=gath.at[grp],
            dst_ref=gath.at[origin],
            send_sem=g_send.at[0],
            recv_sem=g_recv.at[origin],
            device_id=(origin, dev),
            device_id_type=MESH,
        ).wait_recv()

    def far_copy(t):
        return pltpu.make_async_remote_copy(
            src_ref=far.at[dev],
            dst_ref=far.at[dev],
            send_sem=f_send.at[t],
            recv_sem=f_recv.at[dev],
            device_id=(grp, lax.rem(dev + t, peers)),
            device_id_type=MESH,
        )

    def far_arrived(t):
        origin = lax.rem(dev - t + peers, peers)
        pltpu.make_async_remote_copy(
            src_ref=far.at[dev],
            dst_ref=far.at[origin],
            send_sem=f_send.at[0],
            recv_sem=f_recv.at[origin],
            device_id=(grp, origin),
            device_id_type=MESH,
        ).wait_recv()

    scatter_start(
        dot_split(halves(up_t[...]), halves(coef[...])), lift, lift_in, r_send, r_recv
    )

    def near_product(source, weight, first):
        scale = weight * (1.0 / math.sqrt(leaf))

        @pl.loop(0, leaf // row_tile)
        def _(t):
            rows = pl.ds(pl.multiple_of(t * row_tile, row_tile), row_tile)
            squared = None
            for axis in range(3):
                delta = pts_t[rows, axis : axis + 1] - source[axis : axis + 1, :]
                delta = delta - jnp.floor(delta + 0.5)
                squared = delta * delta if squared is None else squared + delta * delta
            block = halves(lax.rsqrt(squared + soften_sq) * scale)
            value = dot_split(block, (xh[...], xl[...]))
            if first:
                out[rows, :] = value
            else:
                out[rows, :] += value

    near_product(pown, 1.0, True)

    def first_relays(begin, end):
        @pl.when(outer)
        def _():
            @pl.loop(begin, end)
            def _(k):
                arrived(slot_of(2), k)
                start_each(first_outer(k))

        @pl.when(inner)
        def _():
            @pl.loop(begin, end)
            def _(k):
                arrived(slot_of(2), k)
                first_inner(k)[1].start()
                arrived(slot_of(3), k)
                first_inner(k)[0].start()

    quarter = chunks // 4
    first_relays(0, quarter)

    gath[grp] = scatter_end(lift, lift_in, r_recv)

    @pl.loop(1, groups)
    def _(t):
        group_copy(t).start()

    first_relays(quarter, 2 * quarter)

    @pl.loop(1, groups)
    def _(t):
        group_arrived(t)

    flat = gath[...].reshape(gath.shape[0] * gath.shape[1], width)
    scatter_start(dot_split(halves(links[...]), halves(flat)), part, part_in, q_send, q_recv)

    first_relays(2 * quarter, 3 * quarter)
    far[dev] = scatter_end(part, part_in, q_recv)

    @pl.loop(1, peers)
    def _(t):
        far_copy(t).start()

    for slot in (0, 1):
        coef_copies[slot].wait_recv()
        coef_copies[slot + 2].start()

    first_relays(3 * quarter, chunks)

    for offset in near_offsets:
        point_copy(offset).wait()

    def add_block(out_offset, in_offset):
        slot = jnp.where(outer, slot_of(out_offset), slot_of(in_offset))
        offset = jnp.where(outer, out_offset, in_offset) * sign
        place_of = jnp.where(offset < 0, offset + 3, offset + 2)
        split_columns(slots.at[slot])
        near_product(pbuf.at[place_of], near_w[place_of], False)

    def wait_for(condition, offset):
        @pl.when(condition)
        def _():
            arrived_all(slot_of(offset))

    wait_for(outer, 1)
    wait_for(inner, -1)
    add_block(1, -1)
    add_block(2, 2)

    @pl.when(outer)
    def _():
        @pl.loop(0, chunks)
        def _(k):
            copies = later_outer(k)
            arrived(slot_of(-2), k)
            copies[0].start()
            arrived(slot_of(-1), k)
            copies[1].start()

    wait_for(outer, 3)
    wait_for(inner, 1)
    add_block(3, 1)
    wait_for(outer, -3)
    add_block(-3, 3)

    @pl.loop(1, peers)
    def _(t):
        far_arrived(t)

    for slot in (2, 3):
        coef_copies[slot].wait_recv()
    total = dot_split(
        halves(up[...]), halves(far[...].reshape(far.shape[0] * far.shape[1], width))
    )
    for entry in range(4):
        total += far_w[entry] * dot_split(halves(coupling[entry]), halves(cbuf[entry]))
    total = halves(total)

    @pl.loop(0, leaf // row_tile)
    def _(t):
        rows = pl.ds(pl.multiple_of(t * row_tile, row_tile), row_tile)
        out[rows, :] += dot_split(halves(basis[rows, :]), total)

    wait_for(inner, -2)
    add_block(-1, -2)
    wait_for(inner, -3)
    add_block(-2, -3)

    for copy in coef_copies:
        copy.wait_send()

    @pl.loop(1, peers)
    def _(t):
        spread(lift, lift_in, r_send, r_recv, t).wait_send()
        spread(part, part_in, q_send, q_recv, t).wait_send()
        far_copy(t).wait_send()

    @pl.loop(1, groups)
    def _(t):
        group_copy(t).wait_send()

    @pl.when(outer)
    def _():
        @pl.loop(0, chunks)
        def _(k):
            for copy in own_outer(k) + first_outer(k) + later_outer(k):
                copy.wait_send()

    @pl.when(inner)
    def _():
        @pl.loop(0, chunks)
        def _(k):
            for copy in own_inner(k) + first_inner(k):
                copy.wait_send()


def per_device(
    columns, points, basis, transfer, leaf_coupling, group_coupling, near_pairs, far_mask,
    group_link_mask,
):
    groups, peers = lax.axis_size("grp"), lax.axis_size("dev")
    leaves = groups * peers
    me = lax.axis_index("grp") * peers + lax.axis_index("dev")
    leaf, width = columns.shape
    rank = basis.shape[1]
    slice_rows = group_coupling.shape[2]
    padded = -(-slice_rows // 8) * 8
    tall = peers * padded
    entries = []
    for offset in (-3, -2, -1, 1, 2, 3):
        row = me if offset > 0 else (me + offset) % leaves
        entries.append(near_pairs[row, abs(offset) - 1])
    near_w = (jnp.stack(entries) > 0).astype(f32)
    far_w = far_mask[0].astype(f32)
    fill = padded - slice_rows
    up = jnp.pad(
        transfer[0].reshape(rank, peers, slice_rows), ((0, 0), (0, 0), (0, fill))
    ).reshape(rank, tall)
    weights = group_link_mask[0].astype(f32)
    links = (weights[:, None, None] * group_coupling[0]).transpose(2, 0, 1)
    links = jnp.pad(
        links.reshape(peers, slice_rows, groups, slice_rows),
        ((0, 0), (0, fill), (0, 0), (0, fill)),
    ).reshape(tall, groups * padded)
    vmem = pl.BlockSpec(memory_space=pltpu.VMEM)
    smem = pl.BlockSpec(memory_space=pltpu.SMEM)
    dma = pltpu.SemaphoreType.DMA
    slab = pltpu.VMEM((peers, padded, width), f32)
    return pl.pallas_call(
        functools.partial(body, groups, peers),
        out_shape=jax.ShapeDtypeStruct((leaf, width), f32),
        in_specs=[smem, smem] + [vmem] * 9,
        out_specs=vmem,
        scratch_shapes=[
            pltpu.VMEM((6, leaf, width), f32),
            pltpu.VMEM((leaf, width), jnp.bfloat16),
            pltpu.VMEM((leaf, width), jnp.bfloat16),
            pltpu.VMEM((8, leaf), f32),
            pltpu.VMEM((6, 8, leaf), f32),
            pltpu.VMEM((rank, width), f32),
            pltpu.VMEM((4, rank, width), f32),
            slab,
            slab,
            pltpu.VMEM((groups, padded, width), f32),
            slab,
            slab,
            slab,
            dma((7, chunks)),
            dma((6, chunks)),
            dma((6,)),
            dma((6,)),
            dma((4,)),
            dma((4,)),
            dma((peers,)),
            dma((peers,)),
            dma((groups,)),
            dma((groups,)),
            dma((peers,)),
            dma((peers,)),
            dma((peers,)),
            dma((peers,)),
        ],
        compiler_params=pltpu.CompilerParams(
            collective_id=0, has_side_effects=True, vmem_limit_bytes=48 * 1024 * 1024
        ),
    )(
        near_w, far_w, columns, points, points.T, basis, basis.T, up, up.T, leaf_coupling[0],
        links,
    )


def solution(mesh):
    in_specs = (
        P(("grp", "dev"), None),
        P(None, ("grp", "dev")),
        P(("grp", "dev"), None),
        P(("grp", "dev"), None, None),
        P(("grp", "dev"), None, None, None),
        P("grp", None, "dev", None),
        P(),
        P(("grp", "dev"), None),
        P("grp", None),
    )
    return jax.shard_map(
        per_device, mesh=mesh, in_specs=in_specs, out_specs=P(("grp", "dev"), None),
        check_vma=False,
    )
```

```python
import functools
import math

import jax
import jax.numpy as jnp
from jax import lax
from jax.experimental import pallas as pl
from jax.experimental.pallas import tpu as pltpu
from jax.sharding import PartitionSpec as P

soften_sq = 0.0025
chunks = 8
row_tile = 128
f32 = jnp.float32
MESH = pl.DeviceIdType.MESH


def slot_of(offset):
    return offset + 3 if offset < 0 else offset + 2


def halves(value):
    high = value.astype(jnp.bfloat16)
    return high, (value - high.astype(f32)).astype(jnp.bfloat16)


def dot16(left, right):
    return jnp.dot(left, right, preferred_element_type=f32)


def dot_split(left, right):
    lh, ll = left
    rh, rl = right
    return dot16(lh, rh) + dot16(lh, rl) + dot16(ll, rh)


def dot16_t(left, right):
    return lax.dot_general(left, right, (((0,), (0,)), ((), ())), preferred_element_type=f32)


def dot_split_t(left, right):
    lh, ll = left
    rh, rl = right
    return dot16_t(lh, rh) + dot16_t(lh, rl) + dot16_t(ll, rh)


def body(
    groups, peers, near_pairs, far_mask, link_mask, cols, pts, basis_in, up_in, coupling_in,
    links_in, out, own, basis, up, coupling, links, slots, xh, xl, pts_t, pown, pbuf, coef, cbuf,
    lift, lift_in, lift_mid, lift_far, gath, part, part_in, part_mid, part_far, far,
    load_sem, s_send, s_recv, p_send, p_recv, c_send, c_recv, pair_send, pair_recv,
    r_send, r_recv, g_send, g_recv, q_send, q_recv, f_send, f_recv,
):
    leaf, width = cols.shape
    loads = [
        pltpu.make_async_copy(source, target, load_sem.at[n])
        for n, (source, target) in enumerate(
            ((cols, own), (basis_in, basis), (up_in, up), (coupling_in, coupling),
             (links_in, links))
        )
    ]
    for load in loads:
        load.start()
    leaves = groups * peers
    grp, dev = lax.axis_index("grp"), lax.axis_index("dev")
    me = grp * peers + dev
    place = lax.rem(me, 4)
    outer = (place == 0) | (place == 3)
    inner = (place == 1) | (place == 2)
    sign = 1 - 2 * (place // 2)
    step = leaf // chunks

    def device(index):
        index = lax.rem(index + leaves, leaves)
        return (index // peers, lax.rem(index, peers))

    barrier = pltpu.get_barrier_semaphore()
    for offset in (-8, -4, -3, -2, -1, 1, 2, 3, 4, 8):
        pl.semaphore_signal(barrier, inc=1, device_id=device(me + offset), device_id_type=MESH)

    @pl.loop(1, peers)
    def _(t):
        pl.semaphore_signal(
            barrier, inc=1, device_id=(grp, lax.rem(dev + t, peers)), device_id_type=MESH
        )

    @pl.loop(1, groups)
    def _(t):
        pl.semaphore_signal(
            barrier, inc=1, device_id=(lax.rem(grp + t, groups), dev), device_id_type=MESH
        )

    pl.semaphore_wait(barrier, 10 + peers - 1 + groups - 1)

    def piece(k):
        return pl.ds(pl.multiple_of(k * step, step), step)

    def relay(source, k, channel, to, offset):
        slot = slot_of(offset)
        return pltpu.make_async_remote_copy(
            src_ref=source.at[piece(k)],
            dst_ref=slots.at[slot, piece(k)],
            send_sem=s_send.at[channel, k],
            recv_sem=s_recv.at[slot, k],
            device_id=device(me + to * sign),
            device_id_type=MESH,
        )

    def arrived(slot, k):
        pltpu.make_async_remote_copy(
            src_ref=cols.at[piece(k)],
            dst_ref=slots.at[slot, piece(k)],
            send_sem=s_send.at[0, k],
            recv_sem=s_recv.at[slot, k],
            device_id=device(me + 1),
            device_id_type=MESH,
        ).wait_recv()

    def arrived_all(slot):
        @pl.loop(0, chunks)
        def _(k):
            arrived(slot, k)

    def own_outer(k):
        return (
            relay(cols, k, 0, 2, 2),
            relay(cols, k, 1, -3, 3),
            relay(cols, k, 2, 1, -1),
        )

    def own_inner(k):
        return (
            relay(cols, k, 0, 2, 2),
            relay(cols, k, 1, 3, -3),
            relay(cols, k, 2, -1, 1),
        )

    plus2, plus3 = slots.at[slot_of(2)], slots.at[slot_of(3)]
    minus1, minus2 = slots.at[slot_of(-1)], slots.at[slot_of(-2)]

    def first_outer(k):
        return relay(plus2, k, 3, 4, -2), relay(plus2, k, 4, 1, 1)

    def first_inner(k):
        return relay(plus3, k, 3, 2, -1), relay(plus2, k, 4, -1, 3)

    def later_outer(k):
        return relay(minus2, k, 5, 1, -3), relay(minus1, k, 6, 1, -2)

    def start_each(copies):
        for copy in copies:
            copy.start()

    def own_start(begin, end):
        @pl.when(outer)
        def _():
            @pl.loop(begin, end)
            def _(k):
                start_each(own_outer(k))

        @pl.when(inner)
        def _():
            @pl.loop(begin, end)
            def _(k):
                start_each(own_inner(k))

    ahead = 2
    own_start(0, ahead)
    pown[0:3, :] = pts[...]
    pown[3:8, :] = jnp.zeros((5, leaf), f32)

    def point_copy(offset):
        return pltpu.make_async_remote_copy(
            src_ref=pown,
            dst_ref=pbuf.at[slot_of(-offset)],
            send_sem=p_send.at[slot_of(offset)],
            recv_sem=p_recv.at[slot_of(-offset)],
            device_id=device(me + offset),
            device_id_type=MESH,
        )

    near_offsets = (-3, -2, -1, 1, 2, 3)
    for offset in near_offsets:
        point_copy(offset).start()

    def split_columns(source):
        @pl.loop(0, leaf // row_tile)
        def _(t):
            rows = pl.ds(pl.multiple_of(t * row_tile, row_tile), row_tile)
            high, low = halves(source[rows, :])
            xh[rows, :] = high
            xl[rows, :] = low

    loads[0].wait()
    split_columns(own)
    loads[1].wait()
    coef[...] = dot_split_t(halves(basis[...]), (xh[...], xl[...]))

    odd = lax.rem(me // 4, 2)
    toward = 4 - 8 * odd

    def coef_copy(source, channel, slot, to):
        return pltpu.make_async_remote_copy(
            src_ref=source,
            dst_ref=cbuf.at[slot],
            send_sem=c_send.at[channel],
            recv_sem=c_recv.at[slot],
            device_id=device(me + to),
            device_id_type=MESH,
        )

    coef_copies = (
        coef_copy(coef, 0, odd, toward),
        coef_copy(cbuf.at[1 - odd], 1, odd, 2 * toward),
        coef_copy(cbuf.at[0], 2, 2, 1),
        coef_copy(cbuf.at[1], 3, 3, -1),
    )
    coef_copies[0].start()

    def coef_arrived(slot):
        coef_copy(coef, 0, slot, 1).wait_recv()

    core, chip, chips = lax.rem(dev, 2), dev // 2, peers // 2
    other = dev + 1 - 2 * core

    def pair_copy(channel, source, target):
        return pltpu.make_async_remote_copy(
            src_ref=source,
            dst_ref=target,
            send_sem=pair_send.at[channel],
            recv_sem=pair_recv.at[channel],
            device_id=(grp, other),
            device_id_type=MESH,
        )

    pair_copies = (
        pair_copy(0, lift.at[1 - core], lift_in),
        pair_copy(1, part.at[1 - core], part_in),
        pair_copy(2, far.at[core], far.at[core]),
    )

    def spread(source, target, send, recv, t):
        to = lax.rem(chip + t, chips)
        return pltpu.make_async_remote_copy(
            src_ref=source.at[to],
            dst_ref=target.at[chip],
            send_sem=send.at[t],
            recv_sem=recv.at[chip],
            device_id=(grp, 2 * to + core),
            device_id_type=MESH,
        )

    def collect(source, target, send, recv, t):
        origin = lax.rem(chip - t + chips, chips)
        pltpu.make_async_remote_copy(
            src_ref=source.at[0],
            dst_ref=target.at[origin],
            send_sem=send.at[0],
            recv_sem=recv.at[origin],
            device_id=(grp, 2 * origin + core),
            device_id_type=MESH,
        ).wait_recv()
        return target[origin]

    def scatter_pair(value, source, channel):
        value = value.reshape((chips, 2) + source.shape[2:])
        for which in range(2):
            source[which] = value[:, which]
        pair_copies[channel].start()

    def scatter_start(source, arriving, middle, target, send, recv, channel):
        pair_copies[channel].wait_recv()
        middle[...] = source[core] + arriving[...]

        @pl.loop(1, chips)
        def _(t):
            spread(middle, target, send, recv, t).start()

    def scatter_end(middle, target, send, recv):
        return lax.fori_loop(
            1, chips,
            lambda t, total: total + collect(middle, target, send, recv, t), middle[chip],
        )

    def group_copy(t):
        return pltpu.make_async_remote_copy(
            src_ref=gath.at[grp],
            dst_ref=gath.at[grp],
            send_sem=g_send.at[t],
            recv_sem=g_recv.at[grp],
            device_id=(lax.rem(grp + t, groups), dev),
            device_id_type=MESH,
        )

    def group_arrived(t):
        origin = lax.rem(grp - t + groups, groups)
        pltpu.make_async_remote_copy(
            src_ref=gath.at[grp],
            dst_ref=gath.at[origin],
            send_sem=g_send.at[0],
            recv_sem=g_recv.at[origin],
            device_id=(origin, dev),
            device_id_type=MESH,
        ).wait_recv()

    def far_copy(t):
        return pltpu.make_async_remote_copy(
            src_ref=far.at[core, chip],
            dst_ref=far.at[core, chip],
            send_sem=f_send.at[t],
            recv_sem=f_recv.at[chip],
            device_id=(grp, 2 * lax.rem(chip + t, chips) + core),
            device_id_type=MESH,
        )

    def far_arrived(t):
        origin = lax.rem(chip - t + chips, chips)
        pltpu.make_async_remote_copy(
            src_ref=far.at[core, chip],
            dst_ref=far.at[core, origin],
            send_sem=f_send.at[0],
            recv_sem=f_recv.at[origin],
            device_id=(grp, 2 * origin + core),
            device_id_type=MESH,
        ).wait_recv()

    loads[2].wait()
    scatter_pair(dot_split_t(halves(up[...]), halves(coef[...])), lift, 0)
    pts_t[...] = pown[...].T

    def near_product(source, weight, first):
        scale = weight * (1.0 / math.sqrt(leaf))

        @pl.loop(0, leaf // row_tile)
        def _(t):
            rows = pl.ds(pl.multiple_of(t * row_tile, row_tile), row_tile)
            squared = None
            for axis in range(3):
                delta = pts_t[rows, axis : axis + 1] - source[axis : axis + 1, :]
                delta = delta - jnp.floor(delta + 0.5)
                squared = delta * delta if squared is None else squared + delta * delta
            block = halves(lax.rsqrt(squared + soften_sq) * scale)
            value = dot_split(block, (xh[...], xl[...]))
            if first:
                out[rows, :] = value
            else:
                out[rows, :] += value

    near_product(pown, 1.0, True)

    def first_relays(begin, end):
        @pl.when(outer)
        def _():
            @pl.loop(begin, end)
            def _(k):
                arrived(slot_of(2), k)
                start_each(first_outer(k))

        @pl.when(inner)
        def _():
            @pl.loop(begin, end)
            def _(k):
                arrived(slot_of(2), k)
                first_inner(k)[1].start()
                arrived(slot_of(3), k)
                first_inner(k)[0].start()

    def add_block(out_offset, in_offset):
        slot = jnp.where(outer, slot_of(out_offset), slot_of(in_offset))
        offset = jnp.where(outer, out_offset, in_offset) * sign
        place_of = jnp.where(offset < 0, offset + 3, offset + 2)
        row = lax.rem(me + jnp.minimum(offset, 0) + leaves, leaves)
        distance = jnp.maximum(offset, -offset)
        weight = (near_pairs[row, distance - 1] > 0).astype(f32)
        split_columns(slots.at[slot])
        near_product(pbuf.at[place_of], weight, False)

    def wait_for(condition, offset):
        @pl.when(condition)
        def _():
            arrived_all(slot_of(offset))

    def turn(k):
        if k + ahead < chunks:
            own_start(k + ahead, k + ahead + 1)
        first_relays(k, k + 1)

    scatter_start(lift, lift_in, lift_mid, lift_far, r_send, r_recv, 0)
    turn(0)
    gath[grp] = scatter_end(lift_mid, lift_far, r_send, r_recv)

    @pl.loop(1, groups)
    def _(t):
        group_copy(t).start()

    turn(1)
    coef_arrived(1 - odd)
    coef_copies[1].start()

    @pl.loop(1, groups)
    def _(t):
        group_arrived(t)

    for load in loads[3:]:
        load.wait()
    flat = jnp.concatenate(
        [gath[h] * link_mask[0, h].astype(f32) for h in range(groups)], axis=0
    )
    scatter_pair(dot_split_t(halves(links[...]), halves(flat)), part, 1)
    turn(2)
    scatter_start(part, part_in, part_mid, part_far, q_send, q_recv, 1)
    turn(3)
    far[core, chip] = scatter_end(part_mid, part_far, q_send, q_recv)

    @pl.loop(1, chips)
    def _(t):
        far_copy(t).start()

    coef_arrived(odd)
    coef_copies[2].start()
    coef_copies[3].start()
    turn(4)

    @pl.loop(1, chips)
    def _(t):
        far_arrived(t)

    pair_copies[2].start()
    turn(5)
    for offset in near_offsets:
        point_copy(offset).wait()
    wait_for(outer, 1)
    wait_for(inner, -1)
    add_block(1, -1)
    for k in range(6, chunks):
        turn(k)
    add_block(2, 2)

    @pl.when(outer)
    def _():
        @pl.loop(0, chunks)
        def _(k):
            copies = later_outer(k)
            arrived(slot_of(-2), k)
            copies[0].start()
            arrived(slot_of(-1), k)
            copies[1].start()

    wait_for(outer, 3)
    wait_for(inner, 1)
    add_block(3, 1)
    wait_for(outer, -3)
    add_block(-3, 3)

    pair_copies[2].wait_recv()
    for slot in (2, 3):
        coef_arrived(slot)
    raised = jnp.stack([far[0], far[1]], axis=1).reshape(up.shape[1], width)
    total = dot_split(halves(up[...]), halves(raised))
    for entry in range(4):
        total += far_mask[0, entry].astype(f32) * dot_split(halves(coupling[entry]), halves(cbuf[entry]))
    total = halves(total)

    @pl.loop(0, leaf // row_tile)
    def _(t):
        rows = pl.ds(pl.multiple_of(t * row_tile, row_tile), row_tile)
        out[rows, :] += dot_split(halves(basis[rows, :]), total)

    wait_for(inner, -2)
    add_block(-1, -2)
    wait_for(inner, -3)
    add_block(-2, -3)

    for copy in coef_copies + pair_copies:
        copy.wait_send()

    @pl.loop(1, chips)
    def _(t):
        spread(lift_mid, lift_far, r_send, r_recv, t).wait_send()
        spread(part_mid, part_far, q_send, q_recv, t).wait_send()
        far_copy(t).wait_send()

    @pl.loop(1, groups)
    def _(t):
        group_copy(t).wait_send()

    @pl.when(outer)
    def _():
        @pl.loop(0, chunks)
        def _(k):
            for copy in own_outer(k) + first_outer(k) + later_outer(k):
                copy.wait_send()

    @pl.when(inner)
    def _():
        @pl.loop(0, chunks)
        def _(k):
            for copy in own_inner(k) + first_inner(k):
                copy.wait_send()


def per_device(
    columns, points, basis, transfer, leaf_coupling, group_coupling, near_pairs, far_mask,
    group_link_mask,
):
    groups, peers = lax.axis_size("grp"), lax.axis_size("dev")
    leaf, width = columns.shape
    rank = basis.shape[1]
    slice_rows = group_coupling.shape[2]
    padded = -(-slice_rows // 8) * 8
    tall = peers * padded
    fill = padded - slice_rows
    up = transfer[0]
    links = group_coupling[0]
    if fill:
        up = jnp.pad(up.reshape(rank, peers, slice_rows), ((0, 0), (0, 0), (0, fill)))
        links = jnp.pad(
            links.reshape(groups, slice_rows, peers, slice_rows),
            ((0, 0), (0, fill), (0, 0), (0, fill)),
        )
    up = up.reshape(rank, tall)
    links = links.reshape(groups * padded, tall)
    vmem = pl.BlockSpec(memory_space=pltpu.VMEM)
    smem = pl.BlockSpec(memory_space=pltpu.SMEM)
    anywhere = pl.BlockSpec(memory_space=pl.ANY)
    dma = pltpu.SemaphoreType.DMA
    chips = peers // 2
    slab = pltpu.VMEM((chips, padded, width), f32)
    pair = pltpu.VMEM((2, chips, padded, width), f32)
    return pl.pallas_call(
        functools.partial(body, groups, peers),
        out_shape=jax.ShapeDtypeStruct((leaf, width), f32),
        in_specs=[smem] * 3 + [anywhere, vmem] + [anywhere] * 4,
        out_specs=vmem,
        scratch_shapes=[
            pltpu.VMEM((leaf, width), f32),
            pltpu.VMEM((leaf, rank), f32),
            pltpu.VMEM((rank, tall), f32),
            pltpu.VMEM(leaf_coupling.shape[1:], f32),
            pltpu.VMEM((groups * padded, tall), f32),
            pltpu.VMEM((6, leaf, width), f32),
            pltpu.VMEM((leaf, width), jnp.bfloat16),
            pltpu.VMEM((leaf, width), jnp.bfloat16),
            pltpu.VMEM((leaf, 8), f32),
            pltpu.VMEM((8, leaf), f32),
            pltpu.VMEM((6, 8, leaf), f32),
            pltpu.VMEM((rank, width), f32),
            pltpu.VMEM((4, rank, width), f32),
            pair,
            slab,
            slab,
            slab,
            pltpu.VMEM((groups, padded, width), f32),
            pair,
            slab,
            slab,
            slab,
            pair,
            dma((5,)),
            dma((7, chunks)),
            dma((6, chunks)),
            dma((6,)),
            dma((6,)),
            dma((4,)),
            dma((4,)),
            dma((3,)),
            dma((3,)),
            dma((chips,)),
            dma((chips,)),
            dma((groups,)),
            dma((groups,)),
            dma((chips,)),
            dma((chips,)),
            dma((chips,)),
            dma((chips,)),
        ],
        compiler_params=pltpu.CompilerParams(
            collective_id=0, has_side_effects=True, vmem_limit_bytes=48 * 1024 * 1024
        ),
    )(
        near_pairs, far_mask, group_link_mask, columns, points, basis, up, leaf_coupling[0],
        links,
    )


def solution(mesh):
    in_specs = (
        P(("grp", "dev"), None),
        P(None, ("grp", "dev")),
        P(("grp", "dev"), None),
        P(("grp", "dev"), None, None),
        P(("grp", "dev"), None, None, None),
        P("grp", None, "dev", None),
        P(),
        P(("grp", "dev"), None),
        P("grp", None),
    )
    return jax.shard_map(
        per_device, mesh=mesh, in_specs=in_specs, out_specs=P(("grp", "dev"), None),
        check_vma=False,
    )
```

```python
import functools
import math

import jax
import jax.numpy as jnp
from jax import lax
from jax.experimental import pallas as pl
from jax.experimental.pallas import tpu as pltpu
from jax.sharding import PartitionSpec as P

soften_sq = 0.0025
chunks = 16
ahead = 4
lag = 3
row_tile = 128
f32 = jnp.float32
MESH = pl.DeviceIdType.MESH


def slot_of(offset):
    return offset + 3 if offset < 0 else offset + 2


def halves(value):
    high = value.astype(jnp.bfloat16)
    return high, (value - high.astype(f32)).astype(jnp.bfloat16)


def dot16(left, right):
    return jnp.dot(left, right, preferred_element_type=f32)


def dot_split(left, right):
    lh, ll = left
    rh, rl = right
    return dot16(lh, rh) + dot16(lh, rl) + dot16(ll, rh)


def dot16_t(left, right):
    return lax.dot_general(left, right, (((0,), (0,)), ((), ())), preferred_element_type=f32)


def dot_split_t(left, right):
    lh, ll = left
    rh, rl = right
    return dot16_t(lh, rh) + dot16_t(lh, rl) + dot16_t(ll, rh)


def body(
    groups, peers, near_in, far_in, link_in, cols, pts_in, basis_in, up_in, coupling_in,
    links_in, out, near_pairs, far_mask, link_mask, pts, own, basis, up, coupling, links, slots, xh, xl, pts_t, pown, pbuf, coef, cbuf,
    lift, lift_in, lift_mid, lift_far, gath, part, part_in, part_mid, part_far, far,
    load_sem, s_send, s_recv, p_send, p_recv, c_send, c_recv, pair_send, pair_recv,
    r_send, r_recv, g_send, g_recv, q_send, q_recv, f_send, f_recv,
):
    leaf, width = cols.shape
    loads = [
        pltpu.make_async_copy(source, target, load_sem.at[n])
        for n, (source, target) in enumerate(
            ((cols, own), (basis_in, basis), (up_in, up), (coupling_in, coupling),
             (links_in, links), (pts_in, pts), (near_in, near_pairs), (far_in, far_mask),
             (link_in, link_mask))
        )
    ]
    for load in loads:
        load.start()
    leaves = groups * peers
    grp, dev = lax.axis_index("grp"), lax.axis_index("dev")
    me = grp * peers + dev
    place = lax.rem(me, 4)
    outer = (place == 0) | (place == 3)
    inner = (place == 1) | (place == 2)
    sign = 1 - 2 * (place // 2)
    step = leaf // chunks

    def device(index):
        index = lax.rem(index + leaves, leaves)
        return (index // peers, lax.rem(index, peers))

    barrier = pltpu.get_barrier_semaphore()
    for offset in (-8, -4, -3, -2, -1, 1, 2, 3, 4, 8):
        pl.semaphore_signal(barrier, inc=1, device_id=device(me + offset), device_id_type=MESH)

    @pl.loop(1, peers)
    def _(t):
        pl.semaphore_signal(
            barrier, inc=1, device_id=(grp, lax.rem(dev + t, peers)), device_id_type=MESH
        )

    @pl.loop(1, groups)
    def _(t):
        pl.semaphore_signal(
            barrier, inc=1, device_id=(lax.rem(grp + t, groups), dev), device_id_type=MESH
        )

    pl.semaphore_wait(barrier, 10 + peers - 1 + groups - 1)

    def piece(k):
        return pl.ds(pl.multiple_of(k * step, step), step)

    def relay(source, k, channel, to, offset):
        slot = slot_of(offset)
        return pltpu.make_async_remote_copy(
            src_ref=source.at[piece(k)],
            dst_ref=slots.at[slot, piece(k)],
            send_sem=s_send.at[channel, k],
            recv_sem=s_recv.at[slot, k],
            device_id=device(me + to * sign),
            device_id_type=MESH,
        )

    def arrived(slot, k):
        pltpu.make_async_remote_copy(
            src_ref=cols.at[piece(k)],
            dst_ref=slots.at[slot, piece(k)],
            send_sem=s_send.at[0, k],
            recv_sem=s_recv.at[slot, k],
            device_id=device(me + 1),
            device_id_type=MESH,
        ).wait_recv()

    relayed_outer, relayed_inner = (2, -1, -2), (2, 3)

    def wait_for(condition, offset, half):
        @pl.when(condition)
        def _():
            @pl.loop(half * (chunks // 2), (half + 1) * (chunks // 2))
            def _(k):
                arrived(slot_of(offset), k)

    def own_outer(k):
        return (
            relay(cols, k, 0, 2, 2),
            relay(cols, k, 1, -3, 3),
            relay(cols, k, 2, 1, -1),
        )

    def own_inner(k):
        return (
            relay(cols, k, 0, 2, 2),
            relay(cols, k, 1, 3, -3),
            relay(cols, k, 2, -1, 1),
        )

    plus2, plus3 = slots.at[slot_of(2)], slots.at[slot_of(3)]
    minus1, minus2 = slots.at[slot_of(-1)], slots.at[slot_of(-2)]

    def first_outer(k):
        return relay(plus2, k, 3, 4, -2), relay(plus2, k, 4, 1, 1)

    def first_inner(k):
        return relay(plus3, k, 3, 2, -1), relay(plus2, k, 4, -1, 3)

    def later_outer(k):
        return relay(minus2, k, 5, 1, -3), relay(minus1, k, 6, 1, -2)

    def start_each(copies):
        for copy in copies:
            copy.start()

    def own_start(begin, end):
        @pl.when(outer)
        def _():
            @pl.loop(begin, end)
            def _(k):
                start_each(own_outer(k))

        @pl.when(inner)
        def _():
            @pl.loop(begin, end)
            def _(k):
                start_each(own_inner(k))

    own_start(0, ahead)
    loads[5].wait()
    pown[0:3, :] = pts[...]
    pown[3:8, :] = jnp.zeros((5, leaf), f32)

    def point_copy(offset):
        return pltpu.make_async_remote_copy(
            src_ref=pown,
            dst_ref=pbuf.at[slot_of(-offset)],
            send_sem=p_send.at[slot_of(offset)],
            recv_sem=p_recv.at[slot_of(-offset)],
            device_id=device(me + offset),
            device_id_type=MESH,
        )

    near_offsets = (-3, -2, -1, 1, 2, 3)
    for offset in near_offsets:
        point_copy(offset).start()

    half_rows = leaf // 2

    def split_columns(source, begin, end):
        @pl.loop(begin // row_tile, end // row_tile)
        def _(t):
            rows = pl.ds(pl.multiple_of(t * row_tile, row_tile), row_tile)
            high, low = halves(source[rows, :])
            xh[rows, :] = high
            xl[rows, :] = low

    loads[0].wait()
    split_columns(own, 0, leaf)
    loads[1].wait()
    coef[...] = dot_split_t(halves(basis[...]), (xh[...], xl[...]))

    odd = lax.rem(me // 4, 2)
    toward = 4 - 8 * odd

    def coef_copy(source, channel, slot, to):
        return pltpu.make_async_remote_copy(
            src_ref=source,
            dst_ref=cbuf.at[slot],
            send_sem=c_send.at[channel],
            recv_sem=c_recv.at[slot],
            device_id=device(me + to),
            device_id_type=MESH,
        )

    coef_copies = (
        coef_copy(coef, 0, odd, toward),
        coef_copy(cbuf.at[1 - odd], 1, odd, 2 * toward),
        coef_copy(cbuf.at[0], 2, 2, 1),
        coef_copy(cbuf.at[1], 3, 3, -1),
    )
    coef_copies[0].start()

    def coef_arrived(slot):
        coef_copy(coef, 0, slot, 1).wait_recv()

    core, chip, chips = lax.rem(dev, 2), dev // 2, peers // 2
    other = dev + 1 - 2 * core

    def pair_copy(channel, source, target):
        return pltpu.make_async_remote_copy(
            src_ref=source,
            dst_ref=target,
            send_sem=pair_send.at[channel],
            recv_sem=pair_recv.at[channel],
            device_id=(grp, other),
            device_id_type=MESH,
        )

    pair_copies = (
        pair_copy(0, lift.at[1 - core], lift_in),
        pair_copy(1, part.at[1 - core], part_in),
        pair_copy(2, far.at[core], far.at[core]),
    )

    def spread(source, target, send, recv, t):
        to = lax.rem(chip + t, chips)
        return pltpu.make_async_remote_copy(
            src_ref=source.at[to],
            dst_ref=target.at[chip],
            send_sem=send.at[t],
            recv_sem=recv.at[chip],
            device_id=(grp, 2 * to + core),
            device_id_type=MESH,
        )

    def collect(source, target, send, recv, t):
        origin = lax.rem(chip - t + chips, chips)
        pltpu.make_async_remote_copy(
            src_ref=source.at[0],
            dst_ref=target.at[origin],
            send_sem=send.at[0],
            recv_sem=recv.at[origin],
            device_id=(grp, 2 * origin + core),
            device_id_type=MESH,
        ).wait_recv()
        return target[origin]

    def scatter_pair(value, source, channel):
        value = value.reshape((chips, 2) + source.shape[2:])
        for which in range(2):
            source[which] = value[:, which]
        pair_copies[channel].start()

    def scatter_start(source, arriving, middle, target, send, recv, channel):
        pair_copies[channel].wait_recv()
        middle[...] = source[core] + arriving[...]

        @pl.loop(1, chips)
        def _(t):
            spread(middle, target, send, recv, t).start()

    def scatter_end(middle, target, send, recv):
        return lax.fori_loop(
            1, chips,
            lambda t, total: total + collect(middle, target, send, recv, t), middle[chip],
        )

    def group_copy(t):
        return pltpu.make_async_remote_copy(
            src_ref=gath.at[grp],
            dst_ref=gath.at[grp],
            send_sem=g_send.at[t],
            recv_sem=g_recv.at[grp],
            device_id=(lax.rem(grp + t, groups), dev),
            device_id_type=MESH,
        )

    def group_arrived(t):
        origin = lax.rem(grp - t + groups, groups)
        pltpu.make_async_remote_copy(
            src_ref=gath.at[grp],
            dst_ref=gath.at[origin],
            send_sem=g_send.at[0],
            recv_sem=g_recv.at[origin],
            device_id=(origin, dev),
            device_id_type=MESH,
        ).wait_recv()

    def far_copy(t):
        return pltpu.make_async_remote_copy(
            src_ref=far.at[core, chip],
            dst_ref=far.at[core, chip],
            send_sem=f_send.at[t],
            recv_sem=f_recv.at[chip],
            device_id=(grp, 2 * lax.rem(chip + t, chips) + core),
            device_id_type=MESH,
        )

    def far_arrived(t):
        origin = lax.rem(chip - t + chips, chips)
        pltpu.make_async_remote_copy(
            src_ref=far.at[core, chip],
            dst_ref=far.at[core, origin],
            send_sem=f_send.at[0],
            recv_sem=f_recv.at[origin],
            device_id=(grp, 2 * origin + core),
            device_id_type=MESH,
        ).wait_recv()

    loads[2].wait()
    scatter_pair(dot_split_t(halves(up[...]), halves(coef[...])), lift, 0)
    pts_t[...] = pown[...].T

    def near_product(source, weight, begin, end, first):
        scale = weight * (1.0 / math.sqrt(leaf))

        @pl.loop(0, leaf // row_tile)
        def _(t):
            rows = pl.ds(pl.multiple_of(t * row_tile, row_tile), row_tile)
            squared = None
            for axis in range(3):
                delta = pts_t[rows, axis : axis + 1] - source[axis : axis + 1, begin:end]
                delta = delta - jnp.floor(delta + 0.5)
                squared = delta * delta if squared is None else squared + delta * delta
            block = halves(lax.rsqrt(squared + soften_sq) * scale)
            value = dot_split(block, (xh[begin:end, :], xl[begin:end, :]))
            if first:
                out[rows, :] = value
            else:
                out[rows, :] += value

    near_product(pown, 1.0, 0, leaf, True)

    def first_relays(begin, end):
        @pl.when(outer)
        def _():
            @pl.loop(begin, end)
            def _(k):
                arrived(slot_of(2), k)
                start_each(first_outer(k))

        @pl.when(inner)
        def _():
            @pl.loop(begin, end)
            def _(k):
                arrived(slot_of(2), k)
                first_inner(k)[1].start()
                arrived(slot_of(3), k)
                first_inner(k)[0].start()

    def add_half(out_offset, in_offset, half):
        begin = half * half_rows
        end = begin + half_rows
        if out_offset not in relayed_outer:
            wait_for(outer, out_offset, half)
        if in_offset not in relayed_inner:
            wait_for(inner, in_offset, half)
        slot = jnp.where(outer, slot_of(out_offset), slot_of(in_offset))
        offset = jnp.where(outer, out_offset, in_offset) * sign
        place_of = jnp.where(offset < 0, offset + 3, offset + 2)
        row = lax.rem(me + jnp.minimum(offset, 0) + leaves, leaves)
        distance = jnp.maximum(offset, -offset)
        weight = (near_pairs[distance - 1, row] > 0).astype(f32)
        split_columns(slots.at[slot], begin, end)
        near_product(pbuf.at[place_of], weight, begin, end, False)

    def later_relays(begin, end):
        @pl.when(outer)
        def _():
            @pl.loop(begin, end)
            def _(k):
                copies = later_outer(k)
                arrived(slot_of(-2), k)
                copies[0].start()
                arrived(slot_of(-1), k)
                copies[1].start()

    def turns(begin, end):
        for k in range(begin, end):
            if k + ahead < chunks:
                own_start(k + ahead, k + ahead + 1)
            first_relays(k, k + 1)
            if k >= lag:
                later_relays(k - lag, k - lag + 1)

    scatter_start(lift, lift_in, lift_mid, lift_far, r_send, r_recv, 0)
    turns(0, 1)
    gath[grp] = scatter_end(lift_mid, lift_far, r_send, r_recv)

    @pl.loop(1, groups)
    def _(t):
        group_copy(t).start()

    turns(1, 3)
    coef_arrived(1 - odd)
    coef_copies[1].start()

    @pl.loop(1, groups)
    def _(t):
        group_arrived(t)

    for load in loads[3:5] + loads[6:]:
        load.wait()
    flat = jnp.concatenate(
        [gath[h] * link_mask[0, h].astype(f32) for h in range(groups)], axis=0
    )
    scatter_pair(dot_split_t(halves(links[...]), halves(flat)), part, 1)
    turns(3, 4)
    scatter_start(part, part_in, part_mid, part_far, q_send, q_recv, 1)
    turns(4, 6)
    far[core, chip] = scatter_end(part_mid, part_far, q_send, q_recv)

    @pl.loop(1, chips)
    def _(t):
        far_copy(t).start()

    coef_arrived(odd)
    coef_copies[2].start()
    coef_copies[3].start()
    turns(6, 7)

    @pl.loop(1, chips)
    def _(t):
        far_arrived(t)

    pair_copies[2].start()
    turns(7, 8)
    for offset in near_offsets:
        point_copy(offset).wait()
    add_half(1, -1, 0)
    turns(8, 9)
    add_half(2, 2, 0)
    turns(9, 11)
    add_half(3, 1, 0)
    turns(11, 12)
    add_half(-3, 3, 0)
    turns(12, 14)
    add_half(-1, -2, 0)
    turns(14, 15)
    add_half(-2, -3, 0)
    turns(15, chunks)
    add_half(1, -1, 1)
    add_half(2, 2, 1)
    later_relays(chunks - lag, chunks)
    add_half(3, 1, 1)
    add_half(-3, 3, 1)

    pair_copies[2].wait_recv()
    for slot in (2, 3):
        coef_arrived(slot)
    raised = jnp.stack([far[0], far[1]], axis=1).reshape(up.shape[1], width)
    total = dot_split(halves(up[...]), halves(raised))
    for entry in range(4):
        total += far_mask[0, entry].astype(f32) * dot_split(halves(coupling[entry]), halves(cbuf[entry]))
    total = halves(total)

    @pl.loop(0, leaf // row_tile)
    def _(t):
        rows = pl.ds(pl.multiple_of(t * row_tile, row_tile), row_tile)
        out[rows, :] += dot_split(halves(basis[rows, :]), total)

    add_half(-1, -2, 1)
    add_half(-2, -3, 1)

    for copy in coef_copies + pair_copies:
        copy.wait_send()

    @pl.loop(1, chips)
    def _(t):
        spread(lift_mid, lift_far, r_send, r_recv, t).wait_send()
        spread(part_mid, part_far, q_send, q_recv, t).wait_send()
        far_copy(t).wait_send()

    @pl.loop(1, groups)
    def _(t):
        group_copy(t).wait_send()

    @pl.when(outer)
    def _():
        @pl.loop(0, chunks)
        def _(k):
            for copy in own_outer(k) + first_outer(k) + later_outer(k):
                copy.wait_send()

    @pl.when(inner)
    def _():
        @pl.loop(0, chunks)
        def _(k):
            for copy in own_inner(k) + first_inner(k):
                copy.wait_send()


def per_device(
    columns, points, basis, transfer, leaf_coupling, group_coupling, near_pairs, far_mask,
    group_link_mask,
):
    groups, peers = lax.axis_size("grp"), lax.axis_size("dev")
    leaf, width = columns.shape
    rank = basis.shape[1]
    slice_rows = group_coupling.shape[2]
    padded = -(-slice_rows // 8) * 8
    tall = peers * padded
    fill = padded - slice_rows
    up = transfer[0]
    links = group_coupling[0]
    if fill:
        up = jnp.pad(up.reshape(rank, peers, slice_rows), ((0, 0), (0, 0), (0, fill)))
        links = jnp.pad(
            links.reshape(groups, slice_rows, peers, slice_rows),
            ((0, 0), (0, fill), (0, 0), (0, fill)),
        )
    up = up.reshape(rank, tall)
    links = links.reshape(groups * padded, tall)
    vmem = pl.BlockSpec(memory_space=pltpu.VMEM)
    hbm = pl.BlockSpec(memory_space=pltpu.HBM)
    dma = pltpu.SemaphoreType.DMA
    chips = peers // 2
    slab = pltpu.VMEM((chips, padded, width), f32)
    pair = pltpu.VMEM((2, chips, padded, width), f32)
    return pl.pallas_call(
        functools.partial(body, groups, peers),
        out_shape=jax.ShapeDtypeStruct((leaf, width), f32),
        in_specs=[hbm] * 9,
        out_specs=vmem,
        scratch_shapes=[
            pltpu.SMEM(near_pairs.shape[::-1], jnp.int32),
            pltpu.SMEM(far_mask.shape, jnp.int32),
            pltpu.SMEM(group_link_mask.shape, jnp.int32),
            pltpu.VMEM(points.shape, f32),
            pltpu.VMEM((leaf, width), f32),
            pltpu.VMEM((leaf, rank), f32),
            pltpu.VMEM((rank, tall), f32),
            pltpu.VMEM(leaf_coupling.shape[1:], f32),
            pltpu.VMEM((groups * padded, tall), f32),
            pltpu.VMEM((6, leaf, width), f32),
            pltpu.VMEM((leaf, width), jnp.bfloat16),
            pltpu.VMEM((leaf, width), jnp.bfloat16),
            pltpu.VMEM((leaf, 8), f32),
            pltpu.VMEM((8, leaf), f32),
            pltpu.VMEM((6, 8, leaf), f32),
            pltpu.VMEM((rank, width), f32),
            pltpu.VMEM((4, rank, width), f32),
            pair,
            slab,
            slab,
            slab,
            pltpu.VMEM((groups, padded, width), f32),
            pair,
            slab,
            slab,
            slab,
            pair,
            dma((9,)),
            dma((7, chunks)),
            dma((6, chunks)),
            dma((6,)),
            dma((6,)),
            dma((4,)),
            dma((4,)),
            dma((3,)),
            dma((3,)),
            dma((chips,)),
            dma((chips,)),
            dma((groups,)),
            dma((groups,)),
            dma((chips,)),
            dma((chips,)),
            dma((chips,)),
            dma((chips,)),
        ],
        compiler_params=pltpu.CompilerParams(
            collective_id=0, has_side_effects=True, vmem_limit_bytes=62 * 1024 * 1024
        ),
    )(
        near_pairs.T, far_mask, group_link_mask, columns, points, basis, up, leaf_coupling[0],
        links,
    )


def solution(mesh):
    in_specs = (
        P(("grp", "dev"), None),
        P(None, ("grp", "dev")),
        P(("grp", "dev"), None),
        P(("grp", "dev"), None, None),
        P(("grp", "dev"), None, None, None),
        P("grp", None, "dev", None),
        P(),
        P(("grp", "dev"), None),
        P("grp", None),
    )
    return jax.shard_map(
        per_device, mesh=mesh, in_specs=in_specs, out_specs=P(("grp", "dev"), None),
        check_vma=False,
    )
```

```python
import functools
import math

import jax
import jax.numpy as jnp
from jax import lax
from jax.experimental import pallas as pl
from jax.experimental.pallas import tpu as pltpu
from jax.sharding import PartitionSpec as P

soften_sq = 0.0025
chunks = 16
ahead = 3
lag = 4
row_tile = 128
f32 = jnp.float32
MESH = pl.DeviceIdType.MESH


def slot_of(offset):
    return offset + 3 if offset < 0 else offset + 2


def halves(value):
    high = value.astype(jnp.bfloat16)
    return high, (value - high.astype(f32)).astype(jnp.bfloat16)


def dot16(left, right):
    return jnp.dot(left, right, preferred_element_type=f32)


def dot_split(left, right):
    lh, ll = left
    rh, rl = right
    return dot16(lh, rh) + dot16(lh, rl) + dot16(ll, rh)


def dot16_t(left, right):
    return lax.dot_general(left, right, (((0,), (0,)), ((), ())), preferred_element_type=f32)


def dot_split_t(left, right):
    lh, ll = left
    rh, rl = right
    return dot16_t(lh, rh) + dot16_t(lh, rl) + dot16_t(ll, rh)


def body(
    groups, peers, near_in, far_in, link_in, cols, pts_in, basis_in, up_in, coupling_in,
    links_in, out, near_pairs, far_mask, link_mask, pts, own, basis, up, coupling, links, slots, xh, xl, pts_t, pown, pbuf, coef, cbuf,
    lift, lift_in, lift_mid, lift_far, gath, part, part_in, part_mid, part_far, far,
    load_sem, s_send, s_recv, p_send, p_recv, c_send, c_recv, pair_send, pair_recv,
    r_send, r_recv, g_send, g_recv, q_send, q_recv, f_send, f_recv,
):
    leaf, width = cols.shape
    loads = [
        pltpu.make_async_copy(source, target, load_sem.at[n])
        for n, (source, target) in enumerate(
            ((cols, own), (basis_in, basis), (up_in, up), (coupling_in, coupling),
             (links_in, links), (pts_in, pts), (near_in, near_pairs), (far_in, far_mask),
             (link_in, link_mask))
        )
    ]
    for load in loads:
        load.start()
    leaves = groups * peers
    grp, dev = lax.axis_index("grp"), lax.axis_index("dev")
    me = grp * peers + dev
    place = lax.rem(me, 4)
    outer = (place == 0) | (place == 3)
    inner = (place == 1) | (place == 2)
    sign = 1 - 2 * (place // 2)
    step = leaf // chunks

    def device(index):
        index = lax.rem(index + leaves, leaves)
        return (index // peers, lax.rem(index, peers))

    barrier = pltpu.get_barrier_semaphore()
    for offset in (-8, -4, -3, -2, -1, 1, 2, 3, 4, 8):
        pl.semaphore_signal(barrier, inc=1, device_id=device(me + offset), device_id_type=MESH)

    @pl.loop(1, peers)
    def _(t):
        pl.semaphore_signal(
            barrier, inc=1, device_id=(grp, lax.rem(dev + t, peers)), device_id_type=MESH
        )

    @pl.loop(1, groups)
    def _(t):
        pl.semaphore_signal(
            barrier, inc=1, device_id=(lax.rem(grp + t, groups), dev), device_id_type=MESH
        )

    pl.semaphore_wait(barrier, 10 + peers - 1 + groups - 1)

    def piece(k):
        return pl.ds(pl.multiple_of(k * step, step), step)

    def relay(source, k, channel, to, offset):
        slot = slot_of(offset)
        return pltpu.make_async_remote_copy(
            src_ref=source.at[piece(k)],
            dst_ref=slots.at[slot, piece(k)],
            send_sem=s_send.at[channel, k],
            recv_sem=s_recv.at[slot, k],
            device_id=device(me + to * sign),
            device_id_type=MESH,
        )

    def arrived(slot, k):
        pltpu.make_async_remote_copy(
            src_ref=cols.at[piece(k)],
            dst_ref=slots.at[slot, piece(k)],
            send_sem=s_send.at[0, k],
            recv_sem=s_recv.at[slot, k],
            device_id=device(me + 1),
            device_id_type=MESH,
        ).wait_recv()

    relayed_outer, relayed_inner = (2, -1, -2), (2, 3)

    def wait_for(condition, offset, half):
        @pl.when(condition)
        def _():
            @pl.loop(half * (chunks // 2), (half + 1) * (chunks // 2))
            def _(k):
                arrived(slot_of(offset), k)

    def own_outer(k):
        return (
            relay(cols, k, 0, 2, 2),
            relay(cols, k, 1, -3, 3),
            relay(cols, k, 2, 1, -1),
        )

    def own_inner(k):
        return (
            relay(cols, k, 0, 2, 2),
            relay(cols, k, 1, 3, -3),
            relay(cols, k, 2, -1, 1),
        )

    plus2, plus3 = slots.at[slot_of(2)], slots.at[slot_of(3)]
    minus1, minus2 = slots.at[slot_of(-1)], slots.at[slot_of(-2)]

    def first_outer(k):
        return relay(plus2, k, 3, 4, -2), relay(plus2, k, 4, 1, 1)

    def first_inner(k):
        return relay(plus3, k, 3, 2, -1), relay(plus2, k, 4, -1, 3)

    def later_outer(k):
        return relay(minus2, k, 5, 1, -3), relay(minus1, k, 6, 1, -2)

    def start_each(copies):
        for copy in copies:
            copy.start()

    def own_start(begin, end):
        @pl.when(outer)
        def _():
            @pl.loop(begin, end)
            def _(k):
                start_each(own_outer(k))

        @pl.when(inner)
        def _():
            @pl.loop(begin, end)
            def _(k):
                start_each(own_inner(k))

    own_start(0, ahead)
    loads[5].wait()
    pown[0:3, :] = pts[...]
    pown[3:8, :] = jnp.zeros((5, leaf), f32)

    def point_copy(offset):
        return pltpu.make_async_remote_copy(
            src_ref=pown,
            dst_ref=pbuf.at[slot_of(-offset)],
            send_sem=p_send.at[slot_of(offset)],
            recv_sem=p_recv.at[slot_of(-offset)],
            device_id=device(me + offset),
            device_id_type=MESH,
        )

    near_offsets = (-3, -2, -1, 1, 2, 3)
    for offset in near_offsets:
        point_copy(offset).start()

    half_rows = leaf // 2

    def split_columns(source, begin, end):
        @pl.loop(begin // row_tile, end // row_tile)
        def _(t):
            rows = pl.ds(pl.multiple_of(t * row_tile, row_tile), row_tile)
            high, low = halves(source[rows, :])
            xh[rows, :] = high
            xl[rows, :] = low

    loads[0].wait()
    split_columns(own, 0, leaf)
    loads[1].wait()
    coef[...] = dot_split_t(halves(basis[...]), (xh[...], xl[...]))

    odd = lax.rem(me // 4, 2)
    toward = 4 - 8 * odd

    def coef_copy(source, channel, slot, to):
        return pltpu.make_async_remote_copy(
            src_ref=source,
            dst_ref=cbuf.at[slot],
            send_sem=c_send.at[channel],
            recv_sem=c_recv.at[slot],
            device_id=device(me + to),
            device_id_type=MESH,
        )

    coef_copies = (
        coef_copy(coef, 0, odd, toward),
        coef_copy(cbuf.at[1 - odd], 1, odd, 2 * toward),
        coef_copy(cbuf.at[0], 2, 2, 1),
        coef_copy(cbuf.at[1], 3, 3, -1),
    )
    coef_copies[0].start()

    def coef_arrived(slot):
        coef_copy(coef, 0, slot, 1).wait_recv()

    core, chip, chips = lax.rem(dev, 2), dev // 2, peers // 2
    other = dev + 1 - 2 * core

    def pair_copy(channel, source, target):
        return pltpu.make_async_remote_copy(
            src_ref=source,
            dst_ref=target,
            send_sem=pair_send.at[channel],
            recv_sem=pair_recv.at[channel],
            device_id=(grp, other),
            device_id_type=MESH,
        )

    pair_copies = (
        pair_copy(0, lift.at[1 - core], lift_in),
        pair_copy(1, part.at[1 - core], part_in),
        pair_copy(2, far.at[core], far.at[core]),
    )

    def spread(source, target, send, recv, t):
        to = lax.rem(chip + t, chips)
        return pltpu.make_async_remote_copy(
            src_ref=source.at[to],
            dst_ref=target.at[chip],
            send_sem=send.at[t],
            recv_sem=recv.at[chip],
            device_id=(grp, 2 * to + core),
            device_id_type=MESH,
        )

    def collect(source, target, send, recv, t):
        origin = lax.rem(chip - t + chips, chips)
        pltpu.make_async_remote_copy(
            src_ref=source.at[0],
            dst_ref=target.at[origin],
            send_sem=send.at[0],
            recv_sem=recv.at[origin],
            device_id=(grp, 2 * origin + core),
            device_id_type=MESH,
        ).wait_recv()
        return target[origin]

    def scatter_pair(value, source, channel):
        value = value.reshape((chips, 2) + source.shape[2:])
        for which in range(2):
            source[which] = value[:, which]
        pair_copies[channel].start()

    def scatter_start(source, arriving, middle, target, send, recv, channel):
        pair_copies[channel].wait_recv()
        middle[...] = source[core] + arriving[...]

        @pl.loop(1, chips)
        def _(t):
            spread(middle, target, send, recv, t).start()

    def scatter_end(middle, target, send, recv):
        return lax.fori_loop(
            1, chips,
            lambda t, total: total + collect(middle, target, send, recv, t), middle[chip],
        )

    def group_copy(t):
        return pltpu.make_async_remote_copy(
            src_ref=gath.at[grp],
            dst_ref=gath.at[grp],
            send_sem=g_send.at[t],
            recv_sem=g_recv.at[grp],
            device_id=(lax.rem(grp + t, groups), dev),
            device_id_type=MESH,
        )

    def group_arrived(t):
        origin = lax.rem(grp - t + groups, groups)
        pltpu.make_async_remote_copy(
            src_ref=gath.at[grp],
            dst_ref=gath.at[origin],
            send_sem=g_send.at[0],
            recv_sem=g_recv.at[origin],
            device_id=(origin, dev),
            device_id_type=MESH,
        ).wait_recv()

    def far_copy(t):
        return pltpu.make_async_remote_copy(
            src_ref=far.at[core, chip],
            dst_ref=far.at[core, chip],
            send_sem=f_send.at[t],
            recv_sem=f_recv.at[chip],
            device_id=(grp, 2 * lax.rem(chip + t, chips) + core),
            device_id_type=MESH,
        )

    def far_arrived(t):
        origin = lax.rem(chip - t + chips, chips)
        pltpu.make_async_remote_copy(
            src_ref=far.at[core, chip],
            dst_ref=far.at[core, origin],
            send_sem=f_send.at[0],
            recv_sem=f_recv.at[origin],
            device_id=(grp, 2 * origin + core),
            device_id_type=MESH,
        ).wait_recv()

    loads[2].wait()
    scatter_pair(dot_split_t(halves(up[...]), halves(coef[...])), lift, 0)
    pts_t[...] = pown[...].T

    def near_product(source, weight, begin, end, first):
        scale = weight * (1.0 / math.sqrt(leaf))

        @pl.loop(0, leaf // row_tile)
        def _(t):
            rows = pl.ds(pl.multiple_of(t * row_tile, row_tile), row_tile)
            squared = None
            for axis in range(3):
                delta = pts_t[rows, axis : axis + 1] - source[axis : axis + 1, begin:end]
                delta = delta - jnp.floor(delta + 0.5)
                squared = delta * delta if squared is None else squared + delta * delta
            block = halves(lax.rsqrt(squared + soften_sq) * scale)
            value = dot_split(block, (xh[begin:end, :], xl[begin:end, :]))
            if first:
                out[rows, :] = value
            else:
                out[rows, :] += value

    near_product(pown, 1.0, 0, leaf, True)

    def first_relays(begin, end):
        @pl.when(outer)
        def _():
            @pl.loop(begin, end)
            def _(k):
                arrived(slot_of(2), k)
                start_each(first_outer(k))

        @pl.when(inner)
        def _():
            @pl.loop(begin, end)
            def _(k):
                arrived(slot_of(2), k)
                first_inner(k)[1].start()
                arrived(slot_of(3), k)
                first_inner(k)[0].start()

    def add_half(out_offset, in_offset, half):
        begin = half * half_rows
        end = begin + half_rows
        if out_offset not in relayed_outer:
            wait_for(outer, out_offset, half)
        if in_offset not in relayed_inner:
            wait_for(inner, in_offset, half)
        slot = jnp.where(outer, slot_of(out_offset), slot_of(in_offset))
        offset = jnp.where(outer, out_offset, in_offset) * sign
        place_of = jnp.where(offset < 0, offset + 3, offset + 2)
        row = lax.rem(me + jnp.minimum(offset, 0) + leaves, leaves)
        distance = jnp.maximum(offset, -offset)
        weight = (near_pairs[distance - 1, row] > 0).astype(f32)
        split_columns(slots.at[slot], begin, end)
        near_product(pbuf.at[place_of], weight, begin, end, False)

    def later_relays(begin, end):
        @pl.when(outer)
        def _():
            @pl.loop(begin, end)
            def _(k):
                copies = later_outer(k)
                arrived(slot_of(-2), k)
                copies[0].start()
                arrived(slot_of(-1), k)
                copies[1].start()

    def turns(begin, end):
        for k in range(begin, end):
            if k + ahead < chunks:
                own_start(k + ahead, k + ahead + 1)
            first_relays(k, k + 1)
            if k >= lag:
                later_relays(k - lag, k - lag + 1)

    turns(0, 2)
    scatter_start(lift, lift_in, lift_mid, lift_far, r_send, r_recv, 0)
    turns(2, 4)
    gath[grp] = scatter_end(lift_mid, lift_far, r_send, r_recv)

    @pl.loop(1, groups)
    def _(t):
        group_copy(t).start()

    coef_arrived(1 - odd)
    coef_copies[1].start()
    turns(4, 6)

    @pl.loop(1, groups)
    def _(t):
        group_arrived(t)

    for load in loads[3:5] + loads[6:]:
        load.wait()
    flat = jnp.concatenate(
        [gath[h] * link_mask[0, h].astype(f32) for h in range(groups)], axis=0
    )
    scatter_pair(dot_split_t(halves(links[...]), halves(flat)), part, 1)
    turns(6, 8)
    scatter_start(part, part_in, part_mid, part_far, q_send, q_recv, 1)
    for offset in near_offsets:
        point_copy(offset).wait()
    add_half(1, -1, 0)
    turns(8, 9)
    coef_arrived(odd)
    coef_copies[2].start()
    coef_copies[3].start()
    turns(9, 10)
    far[core, chip] = scatter_end(part_mid, part_far, q_send, q_recv)

    @pl.loop(1, chips)
    def _(t):
        far_copy(t).start()

    add_half(2, 2, 0)
    turns(10, 12)

    @pl.loop(1, chips)
    def _(t):
        far_arrived(t)

    pair_copies[2].start()
    add_half(3, 1, 0)
    turns(12, 13)
    add_half(-3, 3, 0)
    turns(13, 14)
    add_half(-1, -2, 0)
    turns(14, 15)
    add_half(-2, -3, 0)
    turns(15, chunks)
    add_half(1, -1, 1)
    add_half(2, 2, 1)
    later_relays(chunks - lag, chunks)
    add_half(3, 1, 1)
    add_half(-3, 3, 1)

    pair_copies[2].wait_recv()
    for slot in (2, 3):
        coef_arrived(slot)
    raised = jnp.stack([far[0], far[1]], axis=1).reshape(up.shape[1], width)
    total = dot_split(halves(up[...]), halves(raised))
    for entry in range(4):
        total += far_mask[0, entry].astype(f32) * dot_split(halves(coupling[entry]), halves(cbuf[entry]))
    total = halves(total)

    @pl.loop(0, leaf // row_tile)
    def _(t):
        rows = pl.ds(pl.multiple_of(t * row_tile, row_tile), row_tile)
        out[rows, :] += dot_split(halves(basis[rows, :]), total)

    add_half(-1, -2, 1)
    add_half(-2, -3, 1)

    for copy in coef_copies + pair_copies:
        copy.wait_send()

    @pl.loop(1, chips)
    def _(t):
        spread(lift_mid, lift_far, r_send, r_recv, t).wait_send()
        spread(part_mid, part_far, q_send, q_recv, t).wait_send()
        far_copy(t).wait_send()

    @pl.loop(1, groups)
    def _(t):
        group_copy(t).wait_send()

    @pl.when(outer)
    def _():
        @pl.loop(0, chunks)
        def _(k):
            for copy in own_outer(k) + first_outer(k) + later_outer(k):
                copy.wait_send()

    @pl.when(inner)
    def _():
        @pl.loop(0, chunks)
        def _(k):
            for copy in own_inner(k) + first_inner(k):
                copy.wait_send()


def per_device(
    columns, points, basis, transfer, leaf_coupling, group_coupling, near_pairs, far_mask,
    group_link_mask,
):
    groups, peers = lax.axis_size("grp"), lax.axis_size("dev")
    leaf, width = columns.shape
    rank = basis.shape[1]
    slice_rows = group_coupling.shape[2]
    padded = -(-slice_rows // 8) * 8
    tall = peers * padded
    fill = padded - slice_rows
    up = transfer[0]
    links = group_coupling[0]
    if fill:
        up = jnp.pad(up.reshape(rank, peers, slice_rows), ((0, 0), (0, 0), (0, fill)))
        links = jnp.pad(
            links.reshape(groups, slice_rows, peers, slice_rows),
            ((0, 0), (0, fill), (0, 0), (0, fill)),
        )
    up = up.reshape(rank, tall)
    links = links.reshape(groups * padded, tall)
    vmem = pl.BlockSpec(memory_space=pltpu.VMEM)
    hbm = pl.BlockSpec(memory_space=pltpu.HBM)
    dma = pltpu.SemaphoreType.DMA
    chips = peers // 2
    slab = pltpu.VMEM((chips, padded, width), f32)
    pair = pltpu.VMEM((2, chips, padded, width), f32)
    return pl.pallas_call(
        functools.partial(body, groups, peers),
        out_shape=jax.ShapeDtypeStruct((leaf, width), f32),
        in_specs=[hbm] * 9,
        out_specs=vmem,
        scratch_shapes=[
            pltpu.SMEM(near_pairs.shape[::-1], jnp.int32),
            pltpu.SMEM(far_mask.shape, jnp.int32),
            pltpu.SMEM(group_link_mask.shape, jnp.int32),
            pltpu.VMEM(points.shape, f32),
            pltpu.VMEM((leaf, width), f32),
            pltpu.VMEM((leaf, rank), f32),
            pltpu.VMEM((rank, tall), f32),
            pltpu.VMEM(leaf_coupling.shape[1:], f32),
            pltpu.VMEM((groups * padded, tall), f32),
            pltpu.VMEM((6, leaf, width), f32),
            pltpu.VMEM((leaf, width), jnp.bfloat16),
            pltpu.VMEM((leaf, width), jnp.bfloat16),
            pltpu.VMEM((leaf, 8), f32),
            pltpu.VMEM((8, leaf), f32),
            pltpu.VMEM((6, 8, leaf), f32),
            pltpu.VMEM((rank, width), f32),
            pltpu.VMEM((4, rank, width), f32),
            pair,
            slab,
            slab,
            slab,
            pltpu.VMEM((groups, padded, width), f32),
            pair,
            slab,
            slab,
            slab,
            pair,
            dma((9,)),
            dma((7, chunks)),
            dma((6, chunks)),
            dma((6,)),
            dma((6,)),
            dma((4,)),
            dma((4,)),
            dma((3,)),
            dma((3,)),
            dma((chips,)),
            dma((chips,)),
            dma((groups,)),
            dma((groups,)),
            dma((chips,)),
            dma((chips,)),
            dma((chips,)),
            dma((chips,)),
        ],
        compiler_params=pltpu.CompilerParams(
            collective_id=0, has_side_effects=True, vmem_limit_bytes=62 * 1024 * 1024
        ),
    )(
        near_pairs.T, far_mask, group_link_mask, columns, points, basis, up, leaf_coupling[0],
        links,
    )


def solution(mesh):
    in_specs = (
        P(("grp", "dev"), None),
        P(None, ("grp", "dev")),
        P(("grp", "dev"), None),
        P(("grp", "dev"), None, None),
        P(("grp", "dev"), None, None, None),
        P("grp", None, "dev", None),
        P(),
        P(("grp", "dev"), None),
        P("grp", None),
    )
    return jax.shard_map(
        per_device, mesh=mesh, in_specs=in_specs, out_specs=P(("grp", "dev"), None),
        check_vma=False,
    )
```

```python
import functools
import math

import jax
import jax.numpy as jnp
from jax import lax
from jax.experimental import pallas as pl
from jax.experimental.pallas import tpu as pltpu
from jax.sharding import PartitionSpec as P

soften_sq = 0.0025
chunks = 16
ahead = 3
lag = 4
row_tile = 128
f32 = jnp.float32
MESH = pl.DeviceIdType.MESH


def slot_of(offset):
    return offset + 3 if offset < 0 else offset + 2


def halves(value):
    high = value.astype(jnp.bfloat16)
    return high, (value - high.astype(f32)).astype(jnp.bfloat16)


def dot_split(left, right):
    lh, ll = halves(left)
    rh, rl = halves(right)
    return jnp.dot(
        jnp.concatenate([lh, ll, lh], axis=1),
        jnp.concatenate([rh, rh, rl], axis=0),
        preferred_element_type=f32,
    )


def dot_split_t(left, right):
    lh, ll = halves(left)
    rh, rl = halves(right)
    return dot16_t(
        jnp.concatenate([lh, ll, lh], axis=0), jnp.concatenate([rh, rh, rl], axis=0)
    )


def dot16_t(left, right):
    return lax.dot_general(left, right, (((0,), (0,)), ((), ())), preferred_element_type=f32)


def body(
    groups, peers, near_in, far_in, link_in, cols, pts_in, basis_in, up_in, coupling_in,
    links_in, out, near_pairs, far_mask, link_mask, pts, own, basis, up, coupling, links, slots, xcat, kcat, pts_t, pown, pbuf, coef, cbuf,
    lift, lift_in, lift_mid, lift_far, gath, part, part_in, part_mid, part_far, far,
    load_sem, s_send, s_recv, p_send, p_recv, c_send, c_recv, pair_send, pair_recv,
    r_send, r_recv, g_send, g_recv, q_send, q_recv, f_send, f_recv,
):
    leaf, width = cols.shape
    loads = [
        pltpu.make_async_copy(source, target, load_sem.at[n])
        for n, (source, target) in enumerate(
            ((cols, own), (basis_in, basis), (up_in, up), (coupling_in, coupling),
             (links_in, links), (pts_in, pts), (near_in, near_pairs), (far_in, far_mask),
             (link_in, link_mask))
        )
    ]
    for load in loads:
        load.start()
    leaves = groups * peers
    grp, dev = lax.axis_index("grp"), lax.axis_index("dev")
    me = grp * peers + dev
    place = lax.rem(me, 4)
    outer = (place == 0) | (place == 3)
    inner = (place == 1) | (place == 2)
    sign = 1 - 2 * (place // 2)
    step = leaf // chunks

    def device(index):
        index = lax.rem(index + leaves, leaves)
        return (index // peers, lax.rem(index, peers))

    barrier = pltpu.get_barrier_semaphore()
    for offset in (-8, -4, -3, -2, -1, 1, 2, 3, 4, 8):
        pl.semaphore_signal(barrier, inc=1, device_id=device(me + offset), device_id_type=MESH)

    @pl.loop(1, peers)
    def _(t):
        pl.semaphore_signal(
            barrier, inc=1, device_id=(grp, lax.rem(dev + t, peers)), device_id_type=MESH
        )

    @pl.loop(1, groups)
    def _(t):
        pl.semaphore_signal(
            barrier, inc=1, device_id=(lax.rem(grp + t, groups), dev), device_id_type=MESH
        )

    pl.semaphore_wait(barrier, 10 + peers - 1 + groups - 1)

    def piece(k):
        return pl.ds(pl.multiple_of(k * step, step), step)

    def relay(source, k, channel, to, offset):
        slot = slot_of(offset)
        return pltpu.make_async_remote_copy(
            src_ref=source.at[piece(k)],
            dst_ref=slots.at[slot, piece(k)],
            send_sem=s_send.at[channel, k],
            recv_sem=s_recv.at[slot, k],
            device_id=device(me + to * sign),
            device_id_type=MESH,
        )

    def arrived(slot, k):
        pltpu.make_async_remote_copy(
            src_ref=cols.at[piece(k)],
            dst_ref=slots.at[slot, piece(k)],
            send_sem=s_send.at[0, k],
            recv_sem=s_recv.at[slot, k],
            device_id=device(me + 1),
            device_id_type=MESH,
        ).wait_recv()

    relayed_outer, relayed_inner = (2, -1, -2), (2, 3)

    def wait_for(condition, offset, half):
        @pl.when(condition)
        def _():
            @pl.loop(half * (chunks // 2), (half + 1) * (chunks // 2))
            def _(k):
                arrived(slot_of(offset), k)

    def own_outer(k):
        return (
            relay(cols, k, 0, 2, 2),
            relay(cols, k, 1, -3, 3),
            relay(cols, k, 2, 1, -1),
        )

    def own_inner(k):
        return (
            relay(cols, k, 0, 2, 2),
            relay(cols, k, 1, 3, -3),
            relay(cols, k, 2, -1, 1),
        )

    plus2, plus3 = slots.at[slot_of(2)], slots.at[slot_of(3)]
    minus1, minus2 = slots.at[slot_of(-1)], slots.at[slot_of(-2)]

    def first_outer(k):
        return relay(plus2, k, 3, 4, -2), relay(plus2, k, 4, 1, 1)

    def first_inner(k):
        return relay(plus3, k, 3, 2, -1), relay(plus2, k, 4, -1, 3)

    def later_outer(k):
        return relay(minus2, k, 5, 1, -3), relay(minus1, k, 6, 1, -2)

    def start_each(copies):
        for copy in copies:
            copy.start()

    def own_start(begin, end):
        @pl.when(outer)
        def _():
            @pl.loop(begin, end)
            def _(k):
                start_each(own_outer(k))

        @pl.when(inner)
        def _():
            @pl.loop(begin, end)
            def _(k):
                start_each(own_inner(k))

    own_start(0, ahead)
    loads[5].wait()
    pown[0:3, :] = pts[...]
    pown[3:8, :] = jnp.zeros((5, leaf), f32)

    def point_copy(offset):
        return pltpu.make_async_remote_copy(
            src_ref=pown,
            dst_ref=pbuf.at[slot_of(-offset)],
            send_sem=p_send.at[slot_of(offset)],
            recv_sem=p_recv.at[slot_of(-offset)],
            device_id=device(me + offset),
            device_id_type=MESH,
        )

    near_offsets = (-3, -2, -1, 1, 2, 3)
    for offset in near_offsets:
        point_copy(offset).start()

    half_rows = leaf // 2

    def split_columns(source, begin):
        @pl.loop(0, half_rows // row_tile)
        def _(t):
            at = pl.multiple_of(t * row_tile, row_tile)
            high, low = halves(source[pl.ds(begin + at, row_tile), :])
            xcat[pl.ds(at, row_tile), :] = high
            xcat[pl.ds(half_rows + at, row_tile), :] = high
            xcat[pl.ds(2 * half_rows + at, row_tile), :] = low

    def coef_half(begin):
        high, low = halves(basis[begin : begin + half_rows, :])
        return dot16_t(jnp.concatenate([high, low, high], axis=0), xcat[...])

    loads[0].wait()
    loads[1].wait()
    split_columns(own, 0)
    coef[...] = coef_half(0)
    split_columns(own, half_rows)
    coef[...] += coef_half(half_rows)

    odd = lax.rem(me // 4, 2)
    toward = 4 - 8 * odd

    def coef_copy(source, channel, slot, to):
        return pltpu.make_async_remote_copy(
            src_ref=source,
            dst_ref=cbuf.at[slot],
            send_sem=c_send.at[channel],
            recv_sem=c_recv.at[slot],
            device_id=device(me + to),
            device_id_type=MESH,
        )

    coef_copies = (
        coef_copy(coef, 0, odd, toward),
        coef_copy(cbuf.at[1 - odd], 1, odd, 2 * toward),
        coef_copy(cbuf.at[0], 2, 2, 1),
        coef_copy(cbuf.at[1], 3, 3, -1),
    )
    coef_copies[0].start()

    def coef_arrived(slot):
        coef_copy(coef, 0, slot, 1).wait_recv()

    core, chip, chips = lax.rem(dev, 2), dev // 2, peers // 2
    other = dev + 1 - 2 * core

    def pair_copy(channel, source, target):
        return pltpu.make_async_remote_copy(
            src_ref=source,
            dst_ref=target,
            send_sem=pair_send.at[channel],
            recv_sem=pair_recv.at[channel],
            device_id=(grp, other),
            device_id_type=MESH,
        )

    pair_copies = (
        pair_copy(0, lift.at[1 - core], lift_in),
        pair_copy(1, part.at[1 - core], part_in),
        pair_copy(2, far.at[core], far.at[core]),
    )

    def spread(source, target, send, recv, t):
        to = lax.rem(chip + t, chips)
        return pltpu.make_async_remote_copy(
            src_ref=source.at[to],
            dst_ref=target.at[chip],
            send_sem=send.at[t],
            recv_sem=recv.at[chip],
            device_id=(grp, 2 * to + core),
            device_id_type=MESH,
        )

    def collect(source, target, send, recv, t):
        origin = lax.rem(chip - t + chips, chips)
        pltpu.make_async_remote_copy(
            src_ref=source.at[0],
            dst_ref=target.at[origin],
            send_sem=send.at[0],
            recv_sem=recv.at[origin],
            device_id=(grp, 2 * origin + core),
            device_id_type=MESH,
        ).wait_recv()
        return target[origin]

    def scatter_pair(value, source, channel):
        value = value.reshape((chips, 2) + source.shape[2:])
        for which in range(2):
            source[which] = value[:, which]
        pair_copies[channel].start()

    def scatter_start(source, arriving, middle, target, send, recv, channel):
        pair_copies[channel].wait_recv()
        middle[...] = source[core] + arriving[...]

        @pl.loop(1, chips)
        def _(t):
            spread(middle, target, send, recv, t).start()

    def scatter_end(middle, target, send, recv):
        return lax.fori_loop(
            1, chips,
            lambda t, total: total + collect(middle, target, send, recv, t), middle[chip],
        )

    def group_copy(t):
        return pltpu.make_async_remote_copy(
            src_ref=gath.at[grp],
            dst_ref=gath.at[grp],
            send_sem=g_send.at[t],
            recv_sem=g_recv.at[grp],
            device_id=(lax.rem(grp + t, groups), dev),
            device_id_type=MESH,
        )

    def group_arrived(t):
        origin = lax.rem(grp - t + groups, groups)
        pltpu.make_async_remote_copy(
            src_ref=gath.at[grp],
            dst_ref=gath.at[origin],
            send_sem=g_send.at[0],
            recv_sem=g_recv.at[origin],
            device_id=(origin, dev),
            device_id_type=MESH,
        ).wait_recv()

    def far_copy(t):
        return pltpu.make_async_remote_copy(
            src_ref=far.at[core, chip],
            dst_ref=far.at[core, chip],
            send_sem=f_send.at[t],
            recv_sem=f_recv.at[chip],
            device_id=(grp, 2 * lax.rem(chip + t, chips) + core),
            device_id_type=MESH,
        )

    def far_arrived(t):
        origin = lax.rem(chip - t + chips, chips)
        pltpu.make_async_remote_copy(
            src_ref=far.at[core, chip],
            dst_ref=far.at[core, origin],
            send_sem=f_send.at[0],
            recv_sem=f_recv.at[origin],
            device_id=(grp, 2 * origin + core),
            device_id_type=MESH,
        ).wait_recv()

    loads[2].wait()
    scatter_pair(dot_split_t(up[...], coef[...]), lift, 0)
    pts_t[...] = pown[...].T

    column_tile = 256 if width % 256 == 0 else width

    def near_product(source, shift, weight, begin, first):
        scale = weight * (1.0 / math.sqrt(leaf))
        end = begin + half_rows
        coords = [source[axis : axis + 1, begin:end] for axis in range(3)]
        coords[0] = coords[0] + shift

        @pl.loop(0, leaf // row_tile)
        def _(t):
            rows = pl.ds(pl.multiple_of(t * row_tile, row_tile), row_tile)
            delta = pts_t[rows, 0:1] - coords[0]
            squared = delta * delta
            for axis in (1, 2):
                delta = pts_t[rows, axis : axis + 1] - coords[axis]
                delta = delta - jnp.floor(delta + 0.5)
                squared = squared + delta * delta
            high, low = halves(lax.rsqrt(squared + soften_sq) * scale)
            kcat[rows, 0:half_rows] = high
            kcat[rows, half_rows : 2 * half_rows] = low
            kcat[rows, 2 * half_rows : 3 * half_rows] = high

        @pl.loop(0, width // column_tile)
        def _(t):
            at = pl.ds(pl.multiple_of(t * column_tile, column_tile), column_tile)
            value = jnp.dot(kcat[...], xcat[:, at], preferred_element_type=f32)
            if first:
                out[:, at] = value
            else:
                out[:, at] += value

    near_product(pown, 0.0, 1.0, half_rows, True)
    split_columns(own, 0)
    near_product(pown, 0.0, 1.0, 0, False)

    def first_relays(begin, end):
        @pl.when(outer)
        def _():
            @pl.loop(begin, end)
            def _(k):
                arrived(slot_of(2), k)
                start_each(first_outer(k))

        @pl.when(inner)
        def _():
            @pl.loop(begin, end)
            def _(k):
                arrived(slot_of(2), k)
                first_inner(k)[1].start()
                arrived(slot_of(3), k)
                first_inner(k)[0].start()

    def add_half(out_offset, in_offset, half):
        begin = half * half_rows
        if out_offset not in relayed_outer:
            wait_for(outer, out_offset, half)
        if in_offset not in relayed_inner:
            wait_for(inner, in_offset, half)
        slot = jnp.where(outer, slot_of(out_offset), slot_of(in_offset))
        offset = jnp.where(outer, out_offset, in_offset) * sign
        place_of = jnp.where(offset < 0, offset + 3, offset + 2)
        row = lax.rem(me + jnp.minimum(offset, 0) + leaves, leaves)
        distance = jnp.maximum(offset, -offset)
        weight = (near_pairs[distance - 1, row] > 0).astype(f32)
        split_columns(slots.at[slot], begin)
        beyond = me + offset
        shift = jnp.where(beyond >= leaves, 1.0, jnp.where(beyond < 0, -1.0, 0.0))
        near_product(pbuf.at[place_of], shift, weight, begin, False)

    def later_relays(begin, end):
        @pl.when(outer)
        def _():
            @pl.loop(begin, end)
            def _(k):
                copies = later_outer(k)
                arrived(slot_of(-2), k)
                copies[0].start()
                arrived(slot_of(-1), k)
                copies[1].start()

    def turns(begin, end):
        for k in range(begin, end):
            if k + ahead < chunks:
                own_start(k + ahead, k + ahead + 1)
            first_relays(k, k + 1)
            if k >= lag:
                later_relays(k - lag, k - lag + 1)

    turns(0, 2)
    scatter_start(lift, lift_in, lift_mid, lift_far, r_send, r_recv, 0)
    turns(2, 4)
    gath[grp] = scatter_end(lift_mid, lift_far, r_send, r_recv)

    @pl.loop(1, groups)
    def _(t):
        group_copy(t).start()

    coef_arrived(1 - odd)
    coef_copies[1].start()
    turns(4, 6)

    @pl.loop(1, groups)
    def _(t):
        group_arrived(t)

    for load in loads[3:5] + loads[6:]:
        load.wait()
    flat = jnp.concatenate(
        [gath[h] * link_mask[0, h].astype(f32) for h in range(groups)], axis=0
    )
    scatter_pair(dot_split_t(links[...], flat), part, 1)
    turns(6, 8)
    scatter_start(part, part_in, part_mid, part_far, q_send, q_recv, 1)
    for offset in near_offsets:
        point_copy(offset).wait()
    add_half(1, -1, 0)
    turns(8, 9)
    coef_arrived(odd)
    coef_copies[2].start()
    coef_copies[3].start()
    turns(9, 10)
    far[core, chip] = scatter_end(part_mid, part_far, q_send, q_recv)

    @pl.loop(1, chips)
    def _(t):
        far_copy(t).start()

    add_half(2, 2, 0)
    turns(10, 12)

    @pl.loop(1, chips)
    def _(t):
        far_arrived(t)

    pair_copies[2].start()
    add_half(3, 1, 0)
    turns(12, 13)
    add_half(-3, 3, 0)
    turns(13, 14)
    add_half(-1, -2, 0)
    turns(14, 15)
    add_half(-2, -3, 0)
    turns(15, chunks)
    add_half(1, -1, 1)
    add_half(2, 2, 1)
    later_relays(chunks - lag, chunks)
    add_half(3, 1, 1)
    add_half(-3, 3, 1)

    pair_copies[2].wait_recv()
    for slot in (2, 3):
        coef_arrived(slot)
    raised = jnp.stack([far[0], far[1]], axis=1).reshape(up.shape[1], width)
    total = dot_split(up[...], raised)
    for entry in range(4):
        total += far_mask[0, entry].astype(f32) * dot_split(coupling[entry], cbuf[entry])
    high, low = halves(total)
    total = jnp.concatenate([high, high, low], axis=0)

    @pl.loop(0, leaf // row_tile)
    def _(t):
        rows = pl.ds(pl.multiple_of(t * row_tile, row_tile), row_tile)
        high, low = halves(basis[rows, :])
        left = jnp.concatenate([high, low, high], axis=1)
        out[rows, :] += jnp.dot(left, total, preferred_element_type=f32)

    add_half(-1, -2, 1)
    add_half(-2, -3, 1)

    for copy in coef_copies + pair_copies:
        copy.wait_send()

    @pl.loop(1, chips)
    def _(t):
        spread(lift_mid, lift_far, r_send, r_recv, t).wait_send()
        spread(part_mid, part_far, q_send, q_recv, t).wait_send()
        far_copy(t).wait_send()

    @pl.loop(1, groups)
    def _(t):
        group_copy(t).wait_send()

    @pl.when(outer)
    def _():
        @pl.loop(0, chunks)
        def _(k):
            for copy in own_outer(k) + first_outer(k) + later_outer(k):
                copy.wait_send()

    @pl.when(inner)
    def _():
        @pl.loop(0, chunks)
        def _(k):
            for copy in own_inner(k) + first_inner(k):
                copy.wait_send()


def per_device(
    columns, points, basis, transfer, leaf_coupling, group_coupling, near_pairs, far_mask,
    group_link_mask,
):
    groups, peers = lax.axis_size("grp"), lax.axis_size("dev")
    leaf, width = columns.shape
    rank = basis.shape[1]
    slice_rows = group_coupling.shape[2]
    padded = -(-slice_rows // 8) * 8
    tall = peers * padded
    fill = padded - slice_rows
    up = transfer[0]
    links = group_coupling[0]
    if fill:
        up = jnp.pad(up.reshape(rank, peers, slice_rows), ((0, 0), (0, 0), (0, fill)))
        links = jnp.pad(
            links.reshape(groups, slice_rows, peers, slice_rows),
            ((0, 0), (0, fill), (0, 0), (0, fill)),
        )
    up = up.reshape(rank, tall)
    links = links.reshape(groups * padded, tall)
    vmem = pl.BlockSpec(memory_space=pltpu.VMEM)
    hbm = pl.BlockSpec(memory_space=pltpu.HBM)
    dma = pltpu.SemaphoreType.DMA
    chips = peers // 2
    slab = pltpu.VMEM((chips, padded, width), f32)
    pair = pltpu.VMEM((2, chips, padded, width), f32)
    return pl.pallas_call(
        functools.partial(body, groups, peers),
        out_shape=jax.ShapeDtypeStruct((leaf, width), f32),
        in_specs=[hbm] * 9,
        out_specs=vmem,
        scratch_shapes=[
            pltpu.SMEM(near_pairs.shape[::-1], jnp.int32),
            pltpu.SMEM(far_mask.shape, jnp.int32),
            pltpu.SMEM(group_link_mask.shape, jnp.int32),
            pltpu.VMEM(points.shape, f32),
            pltpu.VMEM((leaf, width), f32),
            pltpu.VMEM((leaf, rank), f32),
            pltpu.VMEM((rank, tall), f32),
            pltpu.VMEM(leaf_coupling.shape[1:], f32),
            pltpu.VMEM((groups * padded, tall), f32),
            pltpu.VMEM((6, leaf, width), f32),
            pltpu.VMEM((3 * leaf // 2, width), jnp.bfloat16),
            pltpu.VMEM((leaf, 3 * leaf // 2), jnp.bfloat16),
            pltpu.VMEM((leaf, 8), f32),
            pltpu.VMEM((8, leaf), f32),
            pltpu.VMEM((6, 8, leaf), f32),
            pltpu.VMEM((rank, width), f32),
            pltpu.VMEM((4, rank, width), f32),
            pair,
            slab,
            slab,
            slab,
            pltpu.VMEM((groups, padded, width), f32),
            pair,
            slab,
            slab,
            slab,
            pair,
            dma((9,)),
            dma((7, chunks)),
            dma((6, chunks)),
            dma((6,)),
            dma((6,)),
            dma((4,)),
            dma((4,)),
            dma((3,)),
            dma((3,)),
            dma((chips,)),
            dma((chips,)),
            dma((groups,)),
            dma((groups,)),
            dma((chips,)),
            dma((chips,)),
            dma((chips,)),
            dma((chips,)),
        ],
        compiler_params=pltpu.CompilerParams(
            collective_id=0, has_side_effects=True, vmem_limit_bytes=62 * 1024 * 1024
        ),
    )(
        near_pairs.T, far_mask, group_link_mask, columns, points, basis, up, leaf_coupling[0],
        links,
    )


def solution(mesh):
    in_specs = (
        P(("grp", "dev"), None),
        P(None, ("grp", "dev")),
        P(("grp", "dev"), None),
        P(("grp", "dev"), None, None),
        P(("grp", "dev"), None, None, None),
        P("grp", None, "dev", None),
        P(),
        P(("grp", "dev"), None),
        P("grp", None),
    )
    return jax.shard_map(
        per_device, mesh=mesh, in_specs=in_specs, out_specs=P(("grp", "dev"), None),
        check_vma=False,
    )
```

```python
import functools
import math

import jax
import jax.numpy as jnp
from jax import lax
from jax.experimental import pallas as pl
from jax.experimental.pallas import tpu as pltpu
from jax.sharding import PartitionSpec as P

soften_sq = 0.0025
chunks = 16
ahead = 6
lag = 5
row_tile = 128
f32 = jnp.float32
MESH = pl.DeviceIdType.MESH


def slot_of(offset):
    return offset + 3 if offset < 0 else offset + 2


def halves(value):
    high = value.astype(jnp.bfloat16)
    return high, (value - high.astype(f32)).astype(jnp.bfloat16)


def dot_split(left, right):
    lh, ll = halves(left)
    rh, rl = halves(right)
    return jnp.dot(
        jnp.concatenate([lh, ll, lh], axis=1),
        jnp.concatenate([rh, rh, rl], axis=0),
        preferred_element_type=f32,
    )


def dot_split_t(left, right):
    lh, ll = halves(left)
    rh, rl = halves(right)
    return dot16_t(
        jnp.concatenate([lh, ll, lh], axis=0), jnp.concatenate([rh, rh, rl], axis=0)
    )


def dot16_t(left, right):
    return lax.dot_general(left, right, (((0,), (0,)), ((), ())), preferred_element_type=f32)


def body(
    groups, peers, near_in, far_in, link_in, cols, pts_in, basis_in, up_in, coupling_in,
    links_in, out, near_pairs, far_mask, link_mask, pts, own, basis, up, coupling, links, slots, xcat, kcat, pts_t, pown, pbuf, coef, cbuf,
    lift, lift_in, lift_mid, lift_far, gath, part, part_in, part_mid, part_far, far,
    load_sem, s_send, s_recv, p_send, p_recv, c_send, c_recv, pair_send, pair_recv,
    r_send, r_recv, g_send, g_recv, q_send, q_recv, f_send, f_recv,
):
    leaf, width = cols.shape
    loads = [
        pltpu.make_async_copy(source, target, load_sem.at[n])
        for n, (source, target) in enumerate(
            ((cols, own), (basis_in, basis), (up_in, up), (coupling_in, coupling),
             (links_in, links), (pts_in, pts), (near_in, near_pairs), (far_in, far_mask),
             (link_in, link_mask))
        )
    ]
    for load in loads:
        load.start()
    leaves = groups * peers
    grp, dev = lax.axis_index("grp"), lax.axis_index("dev")
    me = grp * peers + dev
    place = lax.rem(me, 4)
    outer = (place == 0) | (place == 3)
    inner = (place == 1) | (place == 2)
    sign = 1 - 2 * (place // 2)
    step = leaf // chunks

    def device(index):
        index = lax.rem(index + leaves, leaves)
        return (index // peers, lax.rem(index, peers))

    barrier = pltpu.get_barrier_semaphore()
    for offset in (-8, -5, -4, -3, -2, -1, 1, 2, 3, 4, 5, 8):
        pl.semaphore_signal(barrier, inc=1, device_id=device(me + offset), device_id_type=MESH)

    @pl.loop(1, peers)
    def _(t):
        pl.semaphore_signal(
            barrier, inc=1, device_id=(grp, lax.rem(dev + t, peers)), device_id_type=MESH
        )

    @pl.loop(1, groups)
    def _(t):
        pl.semaphore_signal(
            barrier, inc=1, device_id=(lax.rem(grp + t, groups), dev), device_id_type=MESH
        )

    pl.semaphore_wait(barrier, 12 + peers - 1 + groups - 1)

    def piece(k):
        return pl.ds(pl.multiple_of(k * step, step), step)

    def relay(source, k, channel, to, offset):
        slot = slot_of(offset)
        return pltpu.make_async_remote_copy(
            src_ref=source.at[piece(k)],
            dst_ref=slots.at[slot, piece(k)],
            send_sem=s_send.at[channel, k],
            recv_sem=s_recv.at[slot, k],
            device_id=device(me + to * sign),
            device_id_type=MESH,
        )

    def arrived(slot, k):
        pltpu.make_async_remote_copy(
            src_ref=cols.at[piece(k)],
            dst_ref=slots.at[slot, piece(k)],
            send_sem=s_send.at[0, k],
            recv_sem=s_recv.at[slot, k],
            device_id=device(me + 1),
            device_id_type=MESH,
        ).wait_recv()

    relayed_outer, relayed_inner = (2, -1, -2), (2, 3)

    def wait_for(condition, offset, half):
        @pl.when(condition)
        def _():
            @pl.loop(half * (chunks // 2), (half + 1) * (chunks // 2))
            def _(k):
                arrived(slot_of(offset), k)

    def own_outer(k):
        return (
            relay(cols, k, 0, 2, 2),
            relay(cols, k, 1, -3, 3),
            relay(cols, k, 2, 1, -1),
        )

    def own_inner(k):
        return (
            relay(cols, k, 0, 2, 2),
            relay(cols, k, 1, 3, -3),
            relay(cols, k, 2, -1, 1),
        )

    plus2, plus3 = slots.at[slot_of(2)], slots.at[slot_of(3)]
    minus1, minus2 = slots.at[slot_of(-1)], slots.at[slot_of(-2)]

    def first_outer(k):
        return relay(plus2, k, 3, 4, -2), relay(plus2, k, 4, 1, 1)

    def first_inner(k):
        return relay(plus3, k, 3, 2, -1), relay(plus2, k, 4, -1, 3)

    def later_outer(k):
        return relay(minus2, k, 5, 1, -3), relay(minus1, k, 6, 1, -2)

    def start_each(copies):
        for copy in copies:
            copy.start()

    def own_start(begin, end):
        @pl.when(outer)
        def _():
            @pl.loop(begin, end)
            def _(k):
                start_each(own_outer(k))

        @pl.when(inner)
        def _():
            @pl.loop(begin, end)
            def _(k):
                start_each(own_inner(k))

    own_start(0, ahead)
    loads[5].wait()
    pown[0:3, :] = pts[...]
    pown[3:8, :] = jnp.zeros((5, leaf), f32)

    def point_copy(offset):
        return pltpu.make_async_remote_copy(
            src_ref=pown,
            dst_ref=pbuf.at[slot_of(-offset)],
            send_sem=p_send.at[slot_of(offset)],
            recv_sem=p_recv.at[slot_of(-offset)],
            device_id=device(me + offset),
            device_id_type=MESH,
        )

    near_offsets = (-3, -2, -1, 1, 2, 3)
    for offset in near_offsets:
        point_copy(offset).start()

    half_rows = leaf // 2

    def split_columns(source, begin):
        @pl.loop(0, half_rows // row_tile)
        def _(t):
            at = pl.multiple_of(t * row_tile, row_tile)
            high, low = halves(source[pl.ds(begin + at, row_tile), :])
            xcat[pl.ds(at, row_tile), :] = high
            xcat[pl.ds(half_rows + at, row_tile), :] = high
            xcat[pl.ds(2 * half_rows + at, row_tile), :] = low

    def coef_half(begin):
        high, low = halves(basis[begin : begin + half_rows, :])
        return dot16_t(jnp.concatenate([high, low, high], axis=0), xcat[...])

    loads[0].wait()
    loads[1].wait()
    split_columns(own, 0)
    coef[...] = coef_half(0)
    split_columns(own, half_rows)
    coef[...] += coef_half(half_rows)

    odd = lax.rem(me // 4, 2)
    toward = 4 - 8 * odd

    def coef_copy(source, channel, slot, to):
        return pltpu.make_async_remote_copy(
            src_ref=source,
            dst_ref=cbuf.at[slot],
            send_sem=c_send.at[channel],
            recv_sem=c_recv.at[slot],
            device_id=device(me + to),
            device_id_type=MESH,
        )

    coef_copies = (
        coef_copy(coef, 0, odd, toward),
        coef_copy(cbuf.at[1 - odd], 1, odd, 2 * toward),
    )
    rises, falls = place == 3, place == 0

    def far_coef(channel):
        leap, to = ((rises, 1), (falls, -1))[channel - 2]
        return leap, coef_copy(coef, channel, channel, 5 * to), coef_copy(
            cbuf.at[channel - 2], channel, channel, to
        )

    def leap_start(channel):
        leap, direct, _ = far_coef(channel)

        @pl.when(leap)
        def _():
            direct.start()

    def step_start(channel):
        leap, _, via = far_coef(channel)

        @pl.when(jnp.logical_not(leap))
        def _():
            via.start()

    coef_copies[0].start()
    leap_start(2)
    leap_start(3)

    def coef_arrived(slot):
        coef_copy(coef, 0, slot, 1).wait_recv()

    core, chip, chips = lax.rem(dev, 2), dev // 2, peers // 2
    other = dev + 1 - 2 * core

    def pair_copy(channel, source, target):
        return pltpu.make_async_remote_copy(
            src_ref=source,
            dst_ref=target,
            send_sem=pair_send.at[channel],
            recv_sem=pair_recv.at[channel],
            device_id=(grp, other),
            device_id_type=MESH,
        )

    pair_copies = (
        pair_copy(0, lift.at[1 - core], lift_in),
        pair_copy(1, part.at[1 - core], part_in),
        pair_copy(2, far.at[core], far.at[core]),
    )

    def spread(source, target, send, recv, t):
        to = lax.rem(chip + t, chips)
        return pltpu.make_async_remote_copy(
            src_ref=source.at[to],
            dst_ref=target.at[chip],
            send_sem=send.at[t],
            recv_sem=recv.at[chip],
            device_id=(grp, 2 * to + core),
            device_id_type=MESH,
        )

    def collect(source, target, send, recv, t):
        origin = lax.rem(chip - t + chips, chips)
        pltpu.make_async_remote_copy(
            src_ref=source.at[0],
            dst_ref=target.at[origin],
            send_sem=send.at[0],
            recv_sem=recv.at[origin],
            device_id=(grp, 2 * origin + core),
            device_id_type=MESH,
        ).wait_recv()
        return target[origin]

    def scatter_pair(value, source, channel):
        value = value.reshape((chips, 2) + source.shape[2:])
        for which in range(2):
            source[which] = value[:, which]
        pair_copies[channel].start()

    def scatter_start(source, arriving, middle, target, send, recv, channel):
        pair_copies[channel].wait_recv()
        middle[...] = source[core] + arriving[...]

        @pl.loop(1, chips)
        def _(t):
            spread(middle, target, send, recv, t).start()

    def scatter_end(middle, target, send, recv):
        return lax.fori_loop(
            1, chips,
            lambda t, total: total + collect(middle, target, send, recv, t), middle[chip],
        )

    def group_copy(t):
        return pltpu.make_async_remote_copy(
            src_ref=gath.at[grp],
            dst_ref=gath.at[grp],
            send_sem=g_send.at[t],
            recv_sem=g_recv.at[grp],
            device_id=(lax.rem(grp + t, groups), dev),
            device_id_type=MESH,
        )

    def group_arrived(t):
        origin = lax.rem(grp - t + groups, groups)
        pltpu.make_async_remote_copy(
            src_ref=gath.at[grp],
            dst_ref=gath.at[origin],
            send_sem=g_send.at[0],
            recv_sem=g_recv.at[origin],
            device_id=(origin, dev),
            device_id_type=MESH,
        ).wait_recv()

    def far_copy(t):
        return pltpu.make_async_remote_copy(
            src_ref=far.at[core, chip],
            dst_ref=far.at[core, chip],
            send_sem=f_send.at[t],
            recv_sem=f_recv.at[chip],
            device_id=(grp, 2 * lax.rem(chip + t, chips) + core),
            device_id_type=MESH,
        )

    def far_arrived(t):
        origin = lax.rem(chip - t + chips, chips)
        pltpu.make_async_remote_copy(
            src_ref=far.at[core, chip],
            dst_ref=far.at[core, origin],
            send_sem=f_send.at[0],
            recv_sem=f_recv.at[origin],
            device_id=(grp, 2 * origin + core),
            device_id_type=MESH,
        ).wait_recv()

    loads[2].wait()
    scatter_pair(dot_split_t(up[...], coef[...]), lift, 0)
    pts_t[...] = pown[...].T

    column_tile = 256 if width % 256 == 0 else width

    def near_product(source, shift, weight, begin, first):
        scale = weight * (1.0 / math.sqrt(leaf))
        end = begin + half_rows
        coords = [source[axis : axis + 1, begin:end] for axis in range(3)]
        coords[0] = coords[0] + shift

        @pl.loop(0, leaf // row_tile)
        def _(t):
            rows = pl.ds(pl.multiple_of(t * row_tile, row_tile), row_tile)
            delta = pts_t[rows, 0:1] - coords[0]
            squared = delta * delta
            for axis in (1, 2):
                delta = pts_t[rows, axis : axis + 1] - coords[axis]
                delta = delta - jnp.floor(delta + 0.5)
                squared = squared + delta * delta
            high, low = halves(lax.rsqrt(squared + soften_sq) * scale)
            kcat[rows, 0:half_rows] = high
            kcat[rows, half_rows : 2 * half_rows] = low
            kcat[rows, 2 * half_rows : 3 * half_rows] = high

        @pl.loop(0, width // column_tile)
        def _(t):
            at = pl.ds(pl.multiple_of(t * column_tile, column_tile), column_tile)
            value = jnp.dot(kcat[...], xcat[:, at], preferred_element_type=f32)
            if first:
                out[:, at] = value
            else:
                out[:, at] += value

    near_product(pown, 0.0, 1.0, half_rows, True)
    split_columns(own, 0)
    near_product(pown, 0.0, 1.0, 0, False)

    def first_relays(begin, end):
        @pl.when(outer)
        def _():
            @pl.loop(begin, end)
            def _(k):
                arrived(slot_of(2), k)
                start_each(first_outer(k))

        @pl.when(inner)
        def _():
            @pl.loop(begin, end)
            def _(k):
                arrived(slot_of(2), k)
                first_inner(k)[1].start()
                arrived(slot_of(3), k)
                first_inner(k)[0].start()

    def add_half(out_offset, in_offset, half):
        begin = half * half_rows
        if out_offset not in relayed_outer:
            wait_for(outer, out_offset, half)
        if in_offset not in relayed_inner:
            wait_for(inner, in_offset, half)
        slot = jnp.where(outer, slot_of(out_offset), slot_of(in_offset))
        offset = jnp.where(outer, out_offset, in_offset) * sign
        place_of = jnp.where(offset < 0, offset + 3, offset + 2)
        row = lax.rem(me + jnp.minimum(offset, 0) + leaves, leaves)
        distance = jnp.maximum(offset, -offset)
        weight = (near_pairs[distance - 1, row] > 0).astype(f32)
        split_columns(slots.at[slot], begin)
        beyond = me + offset
        shift = jnp.where(beyond >= leaves, 1.0, jnp.where(beyond < 0, -1.0, 0.0))
        near_product(pbuf.at[place_of], shift, weight, begin, False)

    def later_relays(begin, end):
        @pl.when(outer)
        def _():
            @pl.loop(begin, end)
            def _(k):
                copies = later_outer(k)
                arrived(slot_of(-2), k)
                copies[0].start()
                arrived(slot_of(-1), k)
                copies[1].start()

    def turns(begin, end):
        for k in range(begin, end):
            if k + ahead < chunks:
                own_start(k + ahead, k + ahead + 1)
            first_relays(k, k + 1)
            if k >= lag:
                later_relays(k - lag, k - lag + 1)

    turns(0, 2)
    scatter_start(lift, lift_in, lift_mid, lift_far, r_send, r_recv, 0)
    turns(2, 4)
    gath[grp] = scatter_end(lift_mid, lift_far, r_send, r_recv)

    @pl.loop(1, groups)
    def _(t):
        group_copy(t).start()

    coef_arrived(1 - odd)
    coef_copies[1].start()
    turns(4, 6)

    @pl.loop(1, groups)
    def _(t):
        group_arrived(t)

    for load in loads[3:5] + loads[6:]:
        load.wait()
    flat = jnp.concatenate(
        [gath[h] * link_mask[0, h].astype(f32) for h in range(groups)], axis=0
    )
    scatter_pair(dot_split_t(links[...], flat), part, 1)
    turns(6, 8)
    scatter_start(part, part_in, part_mid, part_far, q_send, q_recv, 1)
    for offset in near_offsets:
        point_copy(offset).wait()
    add_half(1, -1, 0)
    turns(8, 9)
    coef_arrived(odd)
    step_start(2)
    step_start(3)
    turns(9, 10)
    far[core, chip] = scatter_end(part_mid, part_far, q_send, q_recv)

    @pl.loop(1, chips)
    def _(t):
        far_copy(t).start()

    add_half(2, 2, 0)
    turns(10, 12)

    @pl.loop(1, chips)
    def _(t):
        far_arrived(t)

    pair_copies[2].start()
    add_half(3, 1, 0)
    turns(12, 13)
    add_half(-3, 3, 0)
    turns(13, 14)
    add_half(-1, -2, 0)
    turns(14, 15)
    add_half(-2, -3, 0)
    turns(15, chunks)
    add_half(1, -1, 1)
    add_half(2, 2, 1)
    later_relays(chunks - lag, chunks)
    add_half(3, 1, 1)
    add_half(-3, 3, 1)

    pair_copies[2].wait_recv()
    for slot in (2, 3):
        coef_arrived(slot)
    raised = jnp.stack([far[0], far[1]], axis=1).reshape(up.shape[1], width)
    total = dot_split(up[...], raised)
    for entry in range(4):
        total += far_mask[0, entry].astype(f32) * dot_split(coupling[entry], cbuf[entry])
    high, low = halves(total)
    total = jnp.concatenate([high, high, low], axis=0)

    @pl.loop(0, leaf // row_tile)
    def _(t):
        rows = pl.ds(pl.multiple_of(t * row_tile, row_tile), row_tile)
        high, low = halves(basis[rows, :])
        left = jnp.concatenate([high, low, high], axis=1)
        out[rows, :] += jnp.dot(left, total, preferred_element_type=f32)

    add_half(-1, -2, 1)
    add_half(-2, -3, 1)

    for copy in coef_copies + pair_copies + (far_coef(2)[1], far_coef(3)[1]):
        copy.wait_send()

    @pl.loop(1, chips)
    def _(t):
        spread(lift_mid, lift_far, r_send, r_recv, t).wait_send()
        spread(part_mid, part_far, q_send, q_recv, t).wait_send()
        far_copy(t).wait_send()

    @pl.loop(1, groups)
    def _(t):
        group_copy(t).wait_send()

    @pl.when(outer)
    def _():
        @pl.loop(0, chunks)
        def _(k):
            for copy in own_outer(k) + first_outer(k) + later_outer(k):
                copy.wait_send()

    @pl.when(inner)
    def _():
        @pl.loop(0, chunks)
        def _(k):
            for copy in own_inner(k) + first_inner(k):
                copy.wait_send()


def per_device(
    columns, points, basis, transfer, leaf_coupling, group_coupling, near_pairs, far_mask,
    group_link_mask,
):
    groups, peers = lax.axis_size("grp"), lax.axis_size("dev")
    leaf, width = columns.shape
    rank = basis.shape[1]
    slice_rows = group_coupling.shape[2]
    padded = -(-slice_rows // 8) * 8
    tall = peers * padded
    fill = padded - slice_rows
    up = transfer[0]
    links = group_coupling[0]
    if fill:
        up = jnp.pad(up.reshape(rank, peers, slice_rows), ((0, 0), (0, 0), (0, fill)))
        links = jnp.pad(
            links.reshape(groups, slice_rows, peers, slice_rows),
            ((0, 0), (0, fill), (0, 0), (0, fill)),
        )
    up = up.reshape(rank, tall)
    links = links.reshape(groups * padded, tall)
    vmem = pl.BlockSpec(memory_space=pltpu.VMEM)
    hbm = pl.BlockSpec(memory_space=pltpu.HBM)
    dma = pltpu.SemaphoreType.DMA
    chips = peers // 2
    slab = pltpu.VMEM((chips, padded, width), f32)
    pair = pltpu.VMEM((2, chips, padded, width), f32)
    return pl.pallas_call(
        functools.partial(body, groups, peers),
        out_shape=jax.ShapeDtypeStruct((leaf, width), f32),
        in_specs=[hbm] * 9,
        out_specs=vmem,
        scratch_shapes=[
            pltpu.SMEM(near_pairs.shape[::-1], jnp.int32),
            pltpu.SMEM(far_mask.shape, jnp.int32),
            pltpu.SMEM(group_link_mask.shape, jnp.int32),
            pltpu.VMEM(points.shape, f32),
            pltpu.VMEM((leaf, width), f32),
            pltpu.VMEM((leaf, rank), f32),
            pltpu.VMEM((rank, tall), f32),
            pltpu.VMEM(leaf_coupling.shape[1:], f32),
            pltpu.VMEM((groups * padded, tall), f32),
            pltpu.VMEM((6, leaf, width), f32),
            pltpu.VMEM((3 * leaf // 2, width), jnp.bfloat16),
            pltpu.VMEM((leaf, 3 * leaf // 2), jnp.bfloat16),
            pltpu.VMEM((leaf, 8), f32),
            pltpu.VMEM((8, leaf), f32),
            pltpu.VMEM((6, 8, leaf), f32),
            pltpu.VMEM((rank, width), f32),
            pltpu.VMEM((4, rank, width), f32),
            pair,
            slab,
            slab,
            slab,
            pltpu.VMEM((groups, padded, width), f32),
            pair,
            slab,
            slab,
            slab,
            pair,
            dma((9,)),
            dma((7, chunks)),
            dma((6, chunks)),
            dma((6,)),
            dma((6,)),
            dma((4,)),
            dma((4,)),
            dma((3,)),
            dma((3,)),
            dma((chips,)),
            dma((chips,)),
            dma((groups,)),
            dma((groups,)),
            dma((chips,)),
            dma((chips,)),
            dma((chips,)),
            dma((chips,)),
        ],
        compiler_params=pltpu.CompilerParams(
            collective_id=0, has_side_effects=True, vmem_limit_bytes=62 * 1024 * 1024
        ),
    )(
        near_pairs.T, far_mask, group_link_mask, columns, points, basis, up, leaf_coupling[0],
        links,
    )


def solution(mesh):
    in_specs = (
        P(("grp", "dev"), None),
        P(None, ("grp", "dev")),
        P(("grp", "dev"), None),
        P(("grp", "dev"), None, None),
        P(("grp", "dev"), None, None, None),
        P("grp", None, "dev", None),
        P(),
        P(("grp", "dev"), None),
        P("grp", None),
    )
    return jax.shard_map(
        per_device, mesh=mesh, in_specs=in_specs, out_specs=P(("grp", "dev"), None),
        check_vma=False,
    )
```

```python
import functools
import math

import jax
import jax.numpy as jnp
from jax import lax
from jax.experimental import pallas as pl
from jax.experimental.pallas import tpu as pltpu
from jax.sharding import PartitionSpec as P

soften_sq = 0.0025
chunks = 16
ahead = 6
lag = 5
row_tile = 128
f32 = jnp.float32
MESH = pl.DeviceIdType.MESH


def slot_of(offset):
    return offset + 3 if offset < 0 else offset + 2


def halves(value):
    high = value.astype(jnp.bfloat16)
    return high, (value - high.astype(f32)).astype(jnp.bfloat16)


def dot_split(left, right):
    lh, ll = halves(left)
    rh, rl = halves(right)
    return jnp.dot(
        jnp.concatenate([lh, ll, lh], axis=1),
        jnp.concatenate([rh, rh, rl], axis=0),
        preferred_element_type=f32,
    )


def dot_split_t(left, right):
    lh, ll = halves(left)
    rh, rl = halves(right)
    return dot16_t(
        jnp.concatenate([lh, ll, lh], axis=0), jnp.concatenate([rh, rh, rl], axis=0)
    )


def dot16_t(left, right):
    return lax.dot_general(left, right, (((0,), (0,)), ((), ())), preferred_element_type=f32)


def body(
    groups, peers, near_in, far_in, link_in, cols, pts_in, basis_in, up_in, coupling_in,
    links_in, out, near_pairs, far_mask, link_mask, pts, own, basis, up, coupling, links, slots, xcat, kcat, pts_t, pown, pbuf, coef, cbuf,
    lift, lift_in, lift_mid, lift_far, gath, part, part_in, part_mid, part_far, far,
    load_sem, s_send, s_recv, p_send, p_recv, c_send, c_recv, pair_send, pair_recv,
    r_send, r_recv, g_send, g_recv, q_send, q_recv, f_send, f_recv,
):
    leaf, width = cols.shape
    loads = [
        pltpu.make_async_copy(source, target, load_sem.at[n])
        for n, (source, target) in enumerate(
            ((cols, own), (basis_in, basis), (up_in, up), (coupling_in, coupling),
             (links_in, links), (pts_in, pts), (near_in, near_pairs), (far_in, far_mask),
             (link_in, link_mask))
        )
    ]
    for load in loads:
        load.start()
    leaves = groups * peers
    grp, dev = lax.axis_index("grp"), lax.axis_index("dev")
    me = grp * peers + dev
    place = lax.rem(me, 4)
    outer = (place == 0) | (place == 3)
    inner = (place == 1) | (place == 2)
    sign = 1 - 2 * (place // 2)
    step = leaf // chunks

    def device(index):
        index = lax.rem(index + leaves, leaves)
        return (index // peers, lax.rem(index, peers))

    barrier = pltpu.get_barrier_semaphore()
    for offset in (-8, -5, -4, -3, -2, -1, 1, 2, 3, 4, 5, 8):
        pl.semaphore_signal(barrier, inc=1, device_id=device(me + offset), device_id_type=MESH)

    @pl.loop(1, peers)
    def _(t):
        pl.semaphore_signal(
            barrier, inc=1, device_id=(grp, lax.rem(dev + t, peers)), device_id_type=MESH
        )

    @pl.loop(1, groups)
    def _(t):
        pl.semaphore_signal(
            barrier, inc=1, device_id=(lax.rem(grp + t, groups), dev), device_id_type=MESH
        )

    pl.semaphore_wait(barrier, 12 + peers - 1 + groups - 1)

    def piece(k):
        return pl.ds(pl.multiple_of(k * step, step), step)

    def relay(source, k, channel, to, offset):
        slot = slot_of(offset)
        return pltpu.make_async_remote_copy(
            src_ref=source.at[piece(k)],
            dst_ref=slots.at[slot, piece(k)],
            send_sem=s_send.at[channel, k],
            recv_sem=s_recv.at[slot, k],
            device_id=device(me + to * sign),
            device_id_type=MESH,
        )

    def arrived(slot, k):
        pltpu.make_async_remote_copy(
            src_ref=cols.at[piece(k)],
            dst_ref=slots.at[slot, piece(k)],
            send_sem=s_send.at[0, k],
            recv_sem=s_recv.at[slot, k],
            device_id=device(me + 1),
            device_id_type=MESH,
        ).wait_recv()

    relayed_outer, relayed_inner = (2, -1, -2), (2, 3)

    def wait_for(condition, offset, half):
        @pl.when(condition)
        def _():
            @pl.loop(half * (chunks // 2), (half + 1) * (chunks // 2))
            def _(k):
                arrived(slot_of(offset), k)

    def own_outer(k):
        return (
            relay(cols, k, 0, 2, 2),
            relay(cols, k, 1, -3, 3),
            relay(cols, k, 2, 1, -1),
        )

    def own_inner(k):
        return (
            relay(cols, k, 0, 2, 2),
            relay(cols, k, 1, 3, -3),
            relay(cols, k, 2, -1, 1),
        )

    plus2, plus3 = slots.at[slot_of(2)], slots.at[slot_of(3)]
    minus1, minus2 = slots.at[slot_of(-1)], slots.at[slot_of(-2)]

    def first_outer(k):
        return relay(plus2, k, 3, 4, -2), relay(plus2, k, 4, 1, 1)

    def first_inner(k):
        return relay(plus3, k, 3, 2, -1), relay(plus2, k, 4, -1, 3)

    def later_outer(k):
        return relay(minus2, k, 5, 1, -3), relay(minus1, k, 6, 1, -2)

    def start_each(copies):
        for copy in copies:
            copy.start()

    def own_start(begin, end):
        @pl.when(outer)
        def _():
            @pl.loop(begin, end)
            def _(k):
                start_each(own_outer(k))

        @pl.when(inner)
        def _():
            @pl.loop(begin, end)
            def _(k):
                start_each(own_inner(k))

    own_start(0, ahead)
    loads[5].wait()
    pown[0:3, :] = pts[...]
    pown[3:8, :] = jnp.zeros((5, leaf), f32)

    def point_copy(offset):
        return pltpu.make_async_remote_copy(
            src_ref=pown,
            dst_ref=pbuf.at[slot_of(-offset)],
            send_sem=p_send.at[slot_of(offset)],
            recv_sem=p_recv.at[slot_of(-offset)],
            device_id=device(me + offset),
            device_id_type=MESH,
        )

    near_offsets = (-3, -2, -1, 1, 2, 3)
    for offset in near_offsets:
        point_copy(offset).start()

    half_rows = leaf // 2

    def split_columns(source, begin):
        @pl.loop(0, half_rows // row_tile)
        def _(t):
            at = pl.multiple_of(t * row_tile, row_tile)
            high, low = halves(source[pl.ds(begin + at, row_tile), :])
            xcat[pl.ds(at, row_tile), :] = high
            xcat[pl.ds(half_rows + at, row_tile), :] = high
            xcat[pl.ds(2 * half_rows + at, row_tile), :] = low

    def coef_half(begin):
        high, low = halves(basis[begin : begin + half_rows, :])
        return dot16_t(jnp.concatenate([high, low, high], axis=0), xcat[...])

    loads[0].wait()
    loads[1].wait()
    split_columns(own, 0)
    coef[...] = coef_half(0)
    split_columns(own, half_rows)
    coef[...] += coef_half(half_rows)

    odd = lax.rem(me // 4, 2)
    toward = 4 - 8 * odd

    def coef_copy(source, channel, slot, to):
        return pltpu.make_async_remote_copy(
            src_ref=source,
            dst_ref=cbuf.at[slot],
            send_sem=c_send.at[channel],
            recv_sem=c_recv.at[slot],
            device_id=device(me + to),
            device_id_type=MESH,
        )

    coef_copies = (
        coef_copy(coef, 0, odd, toward),
        coef_copy(cbuf.at[1 - odd], 1, odd, 2 * toward),
    )
    rises, falls = place == 3, place == 0

    def far_coef(channel):
        leap, to = ((rises, 1), (falls, -1))[channel - 2]
        return leap, coef_copy(coef, channel, channel, 5 * to), coef_copy(
            cbuf.at[channel - 2], channel, channel, to
        )

    def leap_start(channel):
        leap, direct, _ = far_coef(channel)

        @pl.when(leap)
        def _():
            direct.start()

    def step_start(channel):
        leap, _, via = far_coef(channel)

        @pl.when(jnp.logical_not(leap))
        def _():
            via.start()

    coef_copies[0].start()
    leap_start(2)
    leap_start(3)

    def coef_arrived(slot):
        coef_copy(coef, 0, slot, 1).wait_recv()

    core, chip, chips = lax.rem(dev, 2), dev // 2, peers // 2
    other = dev + 1 - 2 * core

    def pair_copy(channel, source, target):
        return pltpu.make_async_remote_copy(
            src_ref=source,
            dst_ref=target,
            send_sem=pair_send.at[channel],
            recv_sem=pair_recv.at[channel],
            device_id=(grp, other),
            device_id_type=MESH,
        )

    pair_copies = (
        pair_copy(0, lift.at[1 - core], lift_in),
        pair_copy(1, part.at[1 - core], part_in),
        pair_copy(2, far.at[core], far.at[core]),
    )

    def spread(source, target, send, recv, t):
        to = lax.rem(chip + t, chips)
        return pltpu.make_async_remote_copy(
            src_ref=source.at[to],
            dst_ref=target.at[chip],
            send_sem=send.at[t],
            recv_sem=recv.at[chip],
            device_id=(grp, 2 * to + core),
            device_id_type=MESH,
        )

    def collect(source, target, send, recv, t):
        origin = lax.rem(chip - t + chips, chips)
        pltpu.make_async_remote_copy(
            src_ref=source.at[0],
            dst_ref=target.at[origin],
            send_sem=send.at[0],
            recv_sem=recv.at[origin],
            device_id=(grp, 2 * origin + core),
            device_id_type=MESH,
        ).wait_recv()
        return target[origin]

    def scatter_pair(value, source, channel):
        value = value.reshape((chips, 2) + source.shape[2:])
        for which in range(2):
            source[which] = value[:, which]
        pair_copies[channel].start()

    def scatter_start(source, arriving, middle, target, send, recv, channel):
        pair_copies[channel].wait_recv()
        middle[...] = source[core] + arriving[...]

        @pl.loop(1, chips)
        def _(t):
            spread(middle, target, send, recv, t).start()

    def scatter_end(middle, target, send, recv):
        return lax.fori_loop(
            1, chips,
            lambda t, total: total + collect(middle, target, send, recv, t), middle[chip],
        )

    def group_copy(t):
        return pltpu.make_async_remote_copy(
            src_ref=gath.at[grp],
            dst_ref=gath.at[grp],
            send_sem=g_send.at[t],
            recv_sem=g_recv.at[grp],
            device_id=(lax.rem(grp + t, groups), dev),
            device_id_type=MESH,
        )

    def group_arrived(t):
        origin = lax.rem(grp - t + groups, groups)
        pltpu.make_async_remote_copy(
            src_ref=gath.at[grp],
            dst_ref=gath.at[origin],
            send_sem=g_send.at[0],
            recv_sem=g_recv.at[origin],
            device_id=(origin, dev),
            device_id_type=MESH,
        ).wait_recv()

    def far_copy(t):
        return pltpu.make_async_remote_copy(
            src_ref=far.at[core, chip],
            dst_ref=far.at[core, chip],
            send_sem=f_send.at[t],
            recv_sem=f_recv.at[chip],
            device_id=(grp, 2 * lax.rem(chip + t, chips) + core),
            device_id_type=MESH,
        )

    def far_arrived(t):
        origin = lax.rem(chip - t + chips, chips)
        pltpu.make_async_remote_copy(
            src_ref=far.at[core, chip],
            dst_ref=far.at[core, origin],
            send_sem=f_send.at[0],
            recv_sem=f_recv.at[origin],
            device_id=(grp, 2 * origin + core),
            device_id_type=MESH,
        ).wait_recv()

    loads[2].wait()
    scatter_pair(dot_split_t(up[...], coef[...]), lift, 0)
    pts_t[...] = pown[...].T

    column_tile = 256 if width % 256 == 0 else width

    def near_product(source, shift, weight, begin, first):
        scale = weight * (1.0 / math.sqrt(leaf))
        end = begin + half_rows
        coords = [source[axis : axis + 1, begin:end] for axis in range(3)]
        coords[0] = coords[0] + shift

        @pl.loop(0, leaf // row_tile)
        def _(t):
            rows = pl.ds(pl.multiple_of(t * row_tile, row_tile), row_tile)
            delta = pts_t[rows, 0:1] - coords[0]
            squared = delta * delta
            for axis in (1, 2):
                delta = pts_t[rows, axis : axis + 1] - coords[axis]
                delta = delta - jnp.floor(delta + 0.5)
                squared = squared + delta * delta
            high, low = halves(lax.rsqrt(squared + soften_sq) * scale)
            kcat[rows, 0:half_rows] = high
            kcat[rows, half_rows : 2 * half_rows] = low
            kcat[rows, 2 * half_rows : 3 * half_rows] = high

        @pl.loop(0, width // column_tile)
        def _(t):
            at = pl.ds(pl.multiple_of(t * column_tile, column_tile), column_tile)
            value = jnp.dot(kcat[...], xcat[:, at], preferred_element_type=f32)
            if first:
                out[:, at] = value
            else:
                out[:, at] += value

    near_product(pown, 0.0, 1.0, half_rows, True)
    split_columns(own, 0)
    near_product(pown, 0.0, 1.0, 0, False)

    def first_relays(begin, end):
        @pl.when(outer)
        def _():
            @pl.loop(begin, end)
            def _(k):
                arrived(slot_of(2), k)
                start_each(first_outer(k))

        @pl.when(inner)
        def _():
            @pl.loop(begin, end)
            def _(k):
                arrived(slot_of(2), k)
                first_inner(k)[1].start()
                arrived(slot_of(3), k)
                first_inner(k)[0].start()

    def add_half(out_offset, in_offset, half):
        begin = half * half_rows
        if out_offset not in relayed_outer:
            wait_for(outer, out_offset, half)
        if in_offset not in relayed_inner:
            wait_for(inner, in_offset, half)
        slot = jnp.where(outer, slot_of(out_offset), slot_of(in_offset))
        offset = jnp.where(outer, out_offset, in_offset) * sign
        place_of = jnp.where(offset < 0, offset + 3, offset + 2)
        row = lax.rem(me + jnp.minimum(offset, 0) + leaves, leaves)
        distance = jnp.maximum(offset, -offset)
        weight = (near_pairs[distance - 1, row] > 0).astype(f32)
        split_columns(slots.at[slot], begin)
        beyond = me + offset
        shift = jnp.where(beyond >= leaves, 1.0, jnp.where(beyond < 0, -1.0, 0.0))
        near_product(pbuf.at[place_of], shift, weight, begin, False)

    def later_relays(begin, end):
        @pl.when(outer)
        def _():
            @pl.loop(begin, end)
            def _(k):
                copies = later_outer(k)
                arrived(slot_of(-2), k)
                copies[0].start()
                arrived(slot_of(-1), k)
                copies[1].start()

    def turns(begin, end):
        for k in range(begin, end):
            if k + ahead < chunks:
                own_start(k + ahead, k + ahead + 1)
            first_relays(k, k + 1)
            if k >= lag:
                later_relays(k - lag, k - lag + 1)

    turns(0, 2)
    scatter_start(lift, lift_in, lift_mid, lift_far, r_send, r_recv, 0)
    turns(2, 4)
    gath[grp] = scatter_end(lift_mid, lift_far, r_send, r_recv)

    @pl.loop(1, groups)
    def _(t):
        group_copy(t).start()

    coef_arrived(1 - odd)
    coef_copies[1].start()
    turns(4, 6)

    @pl.loop(1, groups)
    def _(t):
        group_arrived(t)

    for load in loads[3:5] + loads[6:]:
        load.wait()
    flat = jnp.concatenate(
        [gath[h] * link_mask[0, h].astype(f32) for h in range(groups)], axis=0
    )
    scatter_pair(dot_split_t(links[...], flat), part, 1)
    turns(6, 8)
    scatter_start(part, part_in, part_mid, part_far, q_send, q_recv, 1)
    for offset in near_offsets:
        point_copy(offset).wait()
    add_half(1, -1, 0)
    turns(8, 9)
    coef_arrived(odd)
    step_start(2)
    step_start(3)
    turns(9, 10)
    far[core, chip] = scatter_end(part_mid, part_far, q_send, q_recv)

    @pl.loop(1, chips)
    def _(t):
        far_copy(t).start()

    add_half(2, 2, 0)
    turns(10, 12)

    @pl.loop(1, chips)
    def _(t):
        far_arrived(t)

    pair_copies[2].start()
    add_half(3, 1, 0)
    turns(12, 13)
    add_half(-3, 3, 0)
    turns(13, 14)
    add_half(-1, -2, 0)
    turns(14, 15)
    pair_copies[2].wait_recv()
    for slot in (2, 3):
        coef_arrived(slot)
    raised = jnp.stack([far[0], far[1]], axis=1).reshape(up.shape[1], width)
    total = dot_split(up[...], raised)
    for entry in range(4):
        total += far_mask[0, entry].astype(f32) * dot_split(coupling[entry], cbuf[entry])
    high, low = halves(total)
    total = jnp.concatenate([high, high, low], axis=0)

    @pl.loop(0, leaf // row_tile)
    def _(t):
        rows = pl.ds(pl.multiple_of(t * row_tile, row_tile), row_tile)
        high, low = halves(basis[rows, :])
        left = jnp.concatenate([high, low, high], axis=1)
        out[rows, :] += jnp.dot(left, total, preferred_element_type=f32)

    add_half(-2, -3, 0)
    turns(15, chunks)
    later_relays(chunks - lag, chunks - 3)
    add_half(1, -1, 1)
    later_relays(chunks - 3, chunks - 1)
    add_half(2, 2, 1)
    later_relays(chunks - 1, chunks)
    add_half(3, 1, 1)
    add_half(-3, 3, 1)

    add_half(-1, -2, 1)
    add_half(-2, -3, 1)

    for copy in coef_copies + pair_copies + (far_coef(2)[1], far_coef(3)[1]):
        copy.wait_send()

    @pl.loop(1, chips)
    def _(t):
        spread(lift_mid, lift_far, r_send, r_recv, t).wait_send()
        spread(part_mid, part_far, q_send, q_recv, t).wait_send()
        far_copy(t).wait_send()

    @pl.loop(1, groups)
    def _(t):
        group_copy(t).wait_send()

    @pl.when(outer)
    def _():
        @pl.loop(0, chunks)
        def _(k):
            for copy in own_outer(k) + first_outer(k) + later_outer(k):
                copy.wait_send()

    @pl.when(inner)
    def _():
        @pl.loop(0, chunks)
        def _(k):
            for copy in own_inner(k) + first_inner(k):
                copy.wait_send()


def per_device(
    columns, points, basis, transfer, leaf_coupling, group_coupling, near_pairs, far_mask,
    group_link_mask,
):
    groups, peers = lax.axis_size("grp"), lax.axis_size("dev")
    leaf, width = columns.shape
    rank = basis.shape[1]
    slice_rows = group_coupling.shape[2]
    padded = -(-slice_rows // 8) * 8
    tall = peers * padded
    fill = padded - slice_rows
    up = transfer[0]
    links = group_coupling[0]
    if fill:
        up = jnp.pad(up.reshape(rank, peers, slice_rows), ((0, 0), (0, 0), (0, fill)))
        links = jnp.pad(
            links.reshape(groups, slice_rows, peers, slice_rows),
            ((0, 0), (0, fill), (0, 0), (0, fill)),
        )
    up = up.reshape(rank, tall)
    links = links.reshape(groups * padded, tall)
    vmem = pl.BlockSpec(memory_space=pltpu.VMEM)
    hbm = pl.BlockSpec(memory_space=pltpu.HBM)
    dma = pltpu.SemaphoreType.DMA
    chips = peers // 2
    slab = pltpu.VMEM((chips, padded, width), f32)
    pair = pltpu.VMEM((2, chips, padded, width), f32)
    return pl.pallas_call(
        functools.partial(body, groups, peers),
        out_shape=jax.ShapeDtypeStruct((leaf, width), f32),
        in_specs=[hbm] * 9,
        out_specs=vmem,
        scratch_shapes=[
            pltpu.SMEM(near_pairs.shape[::-1], jnp.int32),
            pltpu.SMEM(far_mask.shape, jnp.int32),
            pltpu.SMEM(group_link_mask.shape, jnp.int32),
            pltpu.VMEM(points.shape, f32),
            pltpu.VMEM((leaf, width), f32),
            pltpu.VMEM((leaf, rank), f32),
            pltpu.VMEM((rank, tall), f32),
            pltpu.VMEM(leaf_coupling.shape[1:], f32),
            pltpu.VMEM((groups * padded, tall), f32),
            pltpu.VMEM((6, leaf, width), f32),
            pltpu.VMEM((3 * leaf // 2, width), jnp.bfloat16),
            pltpu.VMEM((leaf, 3 * leaf // 2), jnp.bfloat16),
            pltpu.VMEM((leaf, 8), f32),
            pltpu.VMEM((8, leaf), f32),
            pltpu.VMEM((6, 8, leaf), f32),
            pltpu.VMEM((rank, width), f32),
            pltpu.VMEM((4, rank, width), f32),
            pair,
            slab,
            slab,
            slab,
            pltpu.VMEM((groups, padded, width), f32),
            pair,
            slab,
            slab,
            slab,
            pair,
            dma((9,)),
            dma((7, chunks)),
            dma((6, chunks)),
            dma((6,)),
            dma((6,)),
            dma((4,)),
            dma((4,)),
            dma((3,)),
            dma((3,)),
            dma((chips,)),
            dma((chips,)),
            dma((groups,)),
            dma((groups,)),
            dma((chips,)),
            dma((chips,)),
            dma((chips,)),
            dma((chips,)),
        ],
        compiler_params=pltpu.CompilerParams(
            collective_id=0, has_side_effects=True, vmem_limit_bytes=62 * 1024 * 1024
        ),
    )(
        near_pairs.T, far_mask, group_link_mask, columns, points, basis, up, leaf_coupling[0],
        links,
    )


def solution(mesh):
    in_specs = (
        P(("grp", "dev"), None),
        P(None, ("grp", "dev")),
        P(("grp", "dev"), None),
        P(("grp", "dev"), None, None),
        P(("grp", "dev"), None, None, None),
        P("grp", None, "dev", None),
        P(),
        P(("grp", "dev"), None),
        P("grp", None),
    )
    return jax.shard_map(
        per_device, mesh=mesh, in_specs=in_specs, out_specs=P(("grp", "dev"), None),
        check_vma=False,
    )
```
